512 devices in a mesh: node: 16 (over y, z_hi, core), group: 32 (over x, z_lo).
Axes of the slice: x: 4, y: 4, z: 16 (z_hi: 2, z_lo: 8; z = z_hi * 8 + z_lo), core: 2. Of those that a mesh axis runs over, the one named last changes fastest.
Arguments:
- residual: bfloat16 [98304, 5120], P(('node', 'group')), may hold values from -24 to 24
- norm_gain_vector: float32 [5120], replicated, may hold values from 0.3 to 3
- key_projection_matrix: bfloat16 [5120, 512], P('node'), may hold values from -0.078125 to 0.078125
- key_output_gradient: bfloat16 [98304, 512], P(('node', 'group')), may hold values from -6 to 6
Outputs:
- residual_gradient: bfloat16 [98304, 5120], P(('node', 'group'))
- weight_grad: float32 [5120, 512], P(('node', 'group'))
The draws below stay inside these ranges and needn't reach their ends.
All inputs are finite; a program needn't handle non-finite values.
Results may differ from the reference program's by a relative error of at most 0.017.
Values may be sent and summed in bfloat16 or wider, within the bound.
A program may use at most 128 MiB of HBM per device.

```python
import math
import jax
import jax.numpy as jnp
from jax import lax

D = 5120
KVW = 512
BLOCK = 128
TOK_DEV = 192
TOKENS = 98304
N_NODE = 16
N_GROUP = 32


def with_spikes(values, own_key, source, target, parts, factor):
    owner, partner = [(jnp.arange(values.shape[position]) // (values.shape[position] // parts)).reshape([-1 if axis == position else 1 for axis in range(values.ndim)]) for position in (source, target)]
    chosen = jax.random.permutation(own_key, parts)[partner]
    strong = (owner == chosen) | (owner == (partner + parts // 2) % parts)
    return jnp.where(strong, factor * values, values)


def level_of(key, dims, split, least, high):
    def one(dim, parts):
        draws = jax.random.uniform(jax.random.fold_in(jax.random.fold_in(key, 6), dim), (parts,), jnp.float32, least / len(split), high / len(split))
        return jnp.repeat(jnp.exp(draws), dims[dim] // parts).reshape((-1,) + (1,) * (len(dims) - dim - 1))

    factor_of = one(*split[0])
    for cut in split[1:]:
        factor_of = factor_of * one(*cut)
    return factor_of


def bell_draw(stream_key, shape, width, most, shards=(), kind=jnp.bfloat16):
    factor_of = level_of(stream_key, shape, shards, -0.22, 0.18) if shards else 1.0
    array = jax.random.normal(stream_key, shape, jnp.float32) * width * factor_of
    return jnp.minimum(jnp.maximum(array, -most), most).astype(kind)


def heavy_noise(key, shape, deviation, bound, cuts, heavy, held_as=jnp.bfloat16):
    drawn = deviation * jax.random.normal(key, shape, jnp.float32)
    if cuts:
        drawn = drawn * level_of(key, shape, cuts, -0.22, 0.18)
    return jnp.clip(with_spikes(drawn, jax.random.fold_in(key, 3), *heavy), -bound, bound).astype(held_as)


def setup_inputs(seed: int = 0) -> dict:
    arg_keys = jax.random.split(jax.random.key(seed), 5)
    residual = heavy_noise(arg_keys[0], (TOKENS, D), 1.0, 24.0, ((0, 512),), (0, 1, 512, 6.0))
    norm_gain_vector = jnp.clip(jnp.exp(jax.random.uniform(arg_keys[1], (D,), jnp.float32, math.log(0.3), math.log(3.0))), 0.3, 3.0)
    key_projection_matrix = bell_draw(arg_keys[2], (D, KVW), D ** -0.5, 0.078125, ((0, 16),))
    key_output_gradient = bell_draw(arg_keys[3], (TOKENS, KVW), 1.0, 6.0, ((0, 512),))
    return {"residual": residual, "norm_gain_vector": norm_gain_vector, "key_projection_matrix": key_projection_matrix, "key_output_gradient": key_output_gradient}


def apply_norm(residual, norm_gain_vector):
    value_entries = residual.astype(jnp.float32)
    root_mean_square = jnp.sqrt(lax.optimization_barrier(jnp.mean(value_entries * value_entries, axis=1, keepdims=True)) + 1e-06)
    unit_input = value_entries / root_mean_square
    normed_input = (unit_input * norm_gain_vector[None, :]).astype(jnp.bfloat16)
    return (unit_input, root_mean_square, normed_input)

def restore(matrix):
    rows = matrix.shape[0]
    blocks = matrix.reshape(rows, matrix.shape[1] // BLOCK, BLOCK)
    scales = ((lax.optimization_barrier(jnp.max(jnp.abs(blocks), axis=2)) + 1e-06) / 127.0).astype(jnp.bfloat16)
    tiles = (blocks / scales.astype(jnp.float32)[:, :, None]).astype(jnp.bfloat16)
    return (tiles.astype(jnp.float32) * scales.astype(jnp.float32)[:, :, None]).reshape(matrix.shape)

def reference(residual, norm_gain_vector, key_projection_matrix, key_output_gradient):
    unit_input, root_mean_square, normed_input = apply_norm(residual, norm_gain_vector)
    feature_grad = lax.dot_general(key_output_gradient, key_projection_matrix, (((1,), (1,)), ((), ())), preferred_element_type=jnp.float32)
    scaled_input = feature_grad * norm_gain_vector[None, :]
    inner_function = lax.optimization_barrier(jnp.mean(scaled_input * unit_input, axis=1, keepdims=True))
    residual_gradient = ((scaled_input - unit_input * inner_function) / root_mean_square).astype(jnp.bfloat16)
    normed_blocks = normed_input.reshape(N_NODE, N_GROUP, TOK_DEV, D)
    cot_blocks = key_output_gradient.reshape(N_NODE, N_GROUP, TOK_DEV, KVW)

    def per_group(total, group_id):

        def per_node(node_id, accum):
            left = lax.dynamic_index_in_dim(lax.dynamic_index_in_dim(normed_blocks, node_id, 0, False), group_id, 0, False)
            right = lax.dynamic_index_in_dim(lax.dynamic_index_in_dim(cot_blocks, node_id, 0, False), group_id, 0, False)
            partial_value = lax.dot_general(left, right, (((0,), (0,)), ((), ())), preferred_element_type=jnp.float32)
            return accum + restore(partial_value)
        first = lax.fori_loop(0, N_NODE, per_node, jnp.zeros((D, KVW), jnp.float32))
        return (total + restore(first), None)
    total, unused = lax.scan(per_group, jnp.zeros((D, KVW), jnp.float32), jnp.arange(N_GROUP, dtype=jnp.int32))
    weight_grad = total * float(TOKENS) ** (-0.5)
    return (residual_gradient, weight_grad)
```

```python
import jax
import jax.numpy as jnp
from jax import lax
from jax.experimental import pallas as pl
from jax.experimental.pallas import tpu as pltpu
from jax.sharding import PartitionSpec as P

MESH = pl.DeviceIdType.MESH
F32, BF16 = jnp.float32, jnp.bfloat16

RING = 4
DEPTH = 16
Z_LO = 8
ORDER = (2, 1, 3, 0)


def place():
    n, g = lax.axis_index("node"), lax.axis_index("group")
    return g // Z_LO, n // 4, (n // 2) % 2 * Z_LO + g % Z_LO, n % 2


def device(x, y, z, c):
    return (y * 4 + z // Z_LO * 2 + c, x * Z_LO + z % Z_LO)


def kernel(
    res_hbm,
    grad_hbm,
    w_hbm,
    gain_ref,
    out_hbm,
    wg_ref,
    res,
    grad,
    both_res,
    both_grad,
    product,
    send1,
    recv1,
    red,
    recv2,
    acc,
    send3,
    recv3,
    w,
    scaled,
    rinv_ref,
    dot_ref,
    out,
    local_sem,
    pair_sem,
    one_sem,
    two_sem,
    three_sem,
    wz_sem,
    wa_sem,
    wb_sem,
    wx_sem,
    wc_sem,
    out_sem,
):
    x, y, z, c = place()
    zh = z // Z_LO
    tokens, width = res.shape
    shard = w_hbm.shape[0]
    quarter = shard // RING
    rows = quarter // Z_LO
    first, second = x + c * (y - x), y + c * (x - y)
    other = device(x, y, z, 1 - c)

    def along_first(d):
        return device((x + (1 - c) * d) % RING, (y + c * d) % RING, z, c)

    def along_second(d):
        return device((x + c * d) % RING, (y + (1 - c) * d) % RING, z, c)

    def along_x(d):
        return device((x + d) % RING, y, z, c)

    def along_y(d):
        return device(x, (y + d) % RING, z, c)

    def along_z(d):
        return device(x, y, (z + d) % DEPTH, c)

    def remote(src, dst, sems, index, target):
        return pltpu.make_async_remote_copy(
            src_ref=src,
            dst_ref=dst,
            send_sem=sems.at[(0, *index)],
            recv_sem=sems.at[(1, *index)],
            device_id=target,
            device_id_type=MESH,
        )

    barrier = pltpu.get_barrier_semaphore()
    partners = (
        [along_z(d) for d in (8, 7, 9, 6, 10, 5, 11, 4, 12, 3, 13, 2, 14, 1, 15)]
        + [along_x(d) for d in (1, 2, 3)]
        + [along_y(d) for d in (1, 2, 3)]
        + [other]
    )
    for partner in partners:
        pl.semaphore_signal(barrier, inc=1, device_id=partner, device_id_type=MESH)

    def w_rows(yy, hi, core, count=shard, at=0):
        start = ((yy * 2 + hi) * 2 + core) * shard + at
        return w.at[pl.ds(pl.multiple_of(start, 16), count)]

    def columns(block, core):
        start = block * (2 * shard) + core * 256
        return res_hbm.at[:, pl.ds(pl.multiple_of(start, 128), 384)]

    mine = pl.ds(pl.multiple_of(c * tokens, 16), tokens)
    load_res = pltpu.make_async_copy(res_hbm, res, local_sem.at[0])
    load_grad = pltpu.make_async_copy(grad_hbm, grad, local_sem.at[1])
    load_w = pltpu.make_async_copy(w_hbm, w_rows(y, zh, c), local_sem.at[2])
    load_pair = [
        pltpu.make_async_copy(columns(b, c), both_res.at[b, mine], local_sem.at[3 + b])
        for b in range(8)
    ]
    load_res.start()
    load_grad.start()
    for b in range(8):
        load_pair[b].start()
    load_w.start()
    load_grad.wait()
    load_res.wait()

    def norm(i, carry):
        at = pl.ds(pl.multiple_of(i * 16, 16), 16)
        v = res[at].astype(F32)
        rms = jnp.sqrt(jnp.sum(v * v, axis=1, keepdims=True) / width + 1e-06)
        rinv = 1.0 / rms
        rinv_ref[at] = jnp.broadcast_to(rinv, (16, 128))
        both_grad[pl.ds(pl.multiple_of(c * tokens + i * 16, 16), 16)] = (
            grad[at].astype(F32) * rinv
        ).astype(BF16)
        return carry

    lax.fori_loop(0, tokens // 16, norm, 0)

    pl.semaphore_wait(barrier, len(partners))

    swap_grad = remote(both_grad.at[mine], both_grad.at[mine], pair_sem, (8,), other)
    swap_res = [
        remote(columns(b, 1 - c), both_res.at[b, mine], pair_sem, (b,), other) for b in range(8)
    ]
    swap_grad.start()
    for b in range(8):
        swap_res[b].start()

    w_far = remote(
        w_hbm.at[pl.ds(pl.multiple_of(x * quarter, 16), quarter)],
        w_rows(y, zh, c, quarter, x * quarter),
        wz_sem,
        (0,),
        along_z(8),
    )
    w_far.start()
    w_near = {d: remote(w_hbm, w_rows(y, zh, c), wa_sem, (d - 1,), along_y(d)) for d in (1, 2, 3)}
    w_near[1].start()
    w_near[3].start()
    load_w.wait()

    def to_other(yy, hi):
        return remote(
            w_rows(yy, hi, c), w_rows(yy, hi, c), wc_sem, (yy * 2 + hi,), other
        )

    to_other(y, zh).start()

    for b in range(8):
        load_pair[b].wait()
    swap_grad.wait_recv()
    for b in range(8):
        swap_res[b].wait_recv()

    def copy_one(d, s):
        return remote(
            send1.at[(first + d) % RING, s], recv1.at[d - 1, s], one_sem, (d - 1, s), along_first(d)
        )

    def partial_block(yy):
        def half(hi, carry):
            product[...] = lax.dot_general(
                both_res[yy * 2 + hi],
                both_grad[...],
                (((0,), (0,)), ((), ())),
                preferred_element_type=F32,
            )
            for q in range(RING):
                at = pl.ds(pl.multiple_of(c * 64 + q * quarter, 16), quarter)
                send1[
                    q + c * (yy - q), yy + c * (q - yy), pl.ds(pl.multiple_of(hi * quarter, 16), quarter)
                ] = product[at].astype(BF16)
            return carry

        lax.fori_loop(0, 2, half, 0)

    for step in ORDER:
        yy = (y + step) % RING
        partial_block(yy)

        @pl.when(c == 0)
        def _(yy=yy):
            for d in (2, 1, 3):
                copy_one(d, yy).start()

    @pl.when(c == 1)
    def _():
        for step in ORDER:
            for d in (2, 1, 3):
                copy_one(d, (x + step) % RING).start()

    w_far.wait_recv()
    lo = 1 - zh

    def w_side(d):
        piece = w_rows(y, lo, c, quarter, x * quarter)
        return remote(piece, piece, wb_sem, (d - 1,), along_y(d))

    for d in (2, 1, 3):
        w_side(d).start()

    def copy_two(e):
        return remote(red.at[(second + e) % RING], recv2.at[e - 1], two_sem, (e - 1,), along_second(e))

    for step in ORDER:
        s = (second + step) % RING
        for d in (1, 2, 3):
            copy_one(d, s).wait_recv()

        def add(i, carry, s=s, step=step):
            at = pl.ds(pl.multiple_of(i * 16, 16), 16)
            total = send1[first, s, at].astype(F32)
            for k in range(3):
                total = total + recv1[k, s, at].astype(F32)
            if step:
                red[s, at] = total.astype(BF16)
            else:
                acc[at] = total
            return carry

        lax.fori_loop(0, 2 * quarter // 16, add, 0)
        if step:
            copy_two(step).start()

    def w_across(d, yy):
        piece = w_rows(yy, lo, c, quarter, x * quarter)
        return remote(piece, piece, wx_sem, (d - 1, yy), along_x(d))

    for d in (1, 2, 3):
        w_side(d).wait_recv()
    for yy in range(RING):
        for d in (2, 1, 3):
            w_across(d, yy).start()
    w_near[2].start()

    dot_ref[...] = jnp.zeros_like(dot_ref)

    def features(block):
        at = pl.ds(pl.multiple_of(block * (2 * shard), 128), 2 * shard)
        value = lax.dot_general(
            grad[...],
            w[pl.ds(pl.multiple_of(block * (2 * shard), 16), 2 * shard)],
            (((1,), (1,)), ((), ())),
            preferred_element_type=F32,
        )
        value = value * gain_ref[:, at]
        scaled[:, at] = value
        dot_ref[...] += jnp.sum(value * res[:, at].astype(F32), axis=1, keepdims=True)

    def from_other(yy, hi):
        remote(
            w_rows(yy, hi, 1 - c), w_rows(yy, hi, 1 - c), wc_sem, (yy * 2 + hi,), other
        ).wait_recv()

    for d in (1, 3):
        w_near[d].wait_recv()
        to_other((y + RING - d) % RING, zh).start()
    for d in (0, 1, 3):
        yy = (y + RING - d) % RING
        from_other(yy, zh)
        features(yy * 2 + zh)

    for e in (1, 3, 2):
        copy_two(e).wait_recv()

    def add_two(i, carry):
        at = pl.ds(pl.multiple_of(i * 16, 16), 16)
        total = acc[at]
        for k in range(3):
            total = total + recv2[k, at].astype(F32)
        acc[at] = total
        return carry

    lax.fori_loop(0, 2 * quarter // 16, add_two, 0)
    acc[2 * quarter :] = jnp.zeros((acc.shape[0] - 2 * quarter, acc.shape[1]), F32)
    for k in range(DEPTH):
        send3[k] = acc[k * rows : k * rows + 16].astype(BF16)

    def copy_three(d):
        return remote(send3.at[(z + d) % DEPTH], recv3.at[d - 1], three_sem, (d - 1,), along_z(d))

    distances = (8, 7, 9, 6, 10, 5, 11, 4, 12, 3, 13, 2, 14, 1, 15)
    for d in distances:
        copy_three(d).start()

    w_near[2].wait_recv()
    to_other((y + 2) % RING, zh).start()
    from_other((y + 2) % RING, zh)
    features((y + 2) % RING * 2 + zh)

    for yy in range(RING):
        for d in (1, 2, 3):
            w_across_in = w_rows(yy, lo, c, quarter, (x + RING - d) % RING * quarter)
            remote(w_across_in, w_across_in, wx_sem, (d - 1, yy), along_x(d)).wait_recv()
        to_other(yy, lo).start()
    for yy in range(RING):
        from_other(yy, lo)
        features(yy * 2 + lo)

    def finish(i, carry):
        at = pl.ds(pl.multiple_of(i * 16, 16), 16)
        rinv = rinv_ref[at][:, :1]
        factor = dot_ref[at][:, :1] * (1.0 / width) * rinv * rinv
        out[at] = ((scaled[at] - res[at].astype(F32) * factor) * rinv).astype(BF16)
        return carry

    lax.fori_loop(0, tokens // 16, finish, 0)
    store = pltpu.make_async_copy(out, out_hbm, out_sem.at[0])
    store.start()

    for d in distances:
        copy_three(d).wait_recv()
    total = send3[z].astype(F32)
    for k in range(DEPTH - 1):
        total = total + recv3[k].astype(F32)
    wg_ref[...] = total

    swap_grad.wait_send()
    for b in range(8):
        swap_res[b].wait_send()
    w_far.wait_send()
    for d in (1, 2, 3):
        w_near[d].wait_send()
        w_side(d).wait_send()
        copy_two(d).wait_send()
        for s in range(RING):
            copy_one(d, s).wait_send()
            w_across(d, s).wait_send()
    for yy in range(RING):
        for hi in range(2):
            to_other(yy, hi).wait_send()
    for d in distances:
        copy_three(d).wait_send()
    store.wait()


def on_device(residual, norm_gain_vector, key_projection_matrix, key_output_gradient):
    tokens, width = residual.shape
    features = key_output_gradient.shape[1]
    shard = key_projection_matrix.shape[0]
    quarter = shard // RING
    hbm = pl.BlockSpec(memory_space=pl.ANY)
    vmem = pl.BlockSpec(memory_space=pltpu.VMEM)
    residual_gradient, sums = pl.pallas_call(
        kernel,
        out_shape=(
            jax.ShapeDtypeStruct((tokens, width), BF16),
            jax.ShapeDtypeStruct((16, features), F32),
        ),
        in_specs=[hbm, hbm, hbm, vmem],
        out_specs=(hbm, vmem),
        scratch_shapes=[
            pltpu.VMEM((tokens, width), BF16),
            pltpu.VMEM((tokens, features), BF16),
            pltpu.VMEM((8, 2 * tokens, 384), BF16),
            pltpu.VMEM((2 * tokens, features), BF16),
            pltpu.VMEM((384, features), F32),
            pltpu.VMEM((RING, RING, 2 * quarter, features), BF16),
            pltpu.VMEM((3, RING, 2 * quarter, features), BF16),
            pltpu.VMEM((RING, 2 * quarter, features), BF16),
            pltpu.VMEM((3, 2 * quarter, features), BF16),
            pltpu.VMEM((2 * quarter + 16, features), F32),
            pltpu.VMEM((DEPTH, 16, features), BF16),
            pltpu.VMEM((DEPTH - 1, 16, features), BF16),
            pltpu.VMEM((width, features), BF16),
            pltpu.VMEM((tokens, width), F32),
            pltpu.VMEM((tokens, 128), F32),
            pltpu.VMEM((tokens, 128), F32),
            pltpu.VMEM((tokens, width), BF16),
            pltpu.SemaphoreType.DMA((11,)),
            pltpu.SemaphoreType.DMA((2, 9)),
            pltpu.SemaphoreType.DMA((2, 3, RING)),
            pltpu.SemaphoreType.DMA((2, 3)),
            pltpu.SemaphoreType.DMA((2, DEPTH - 1)),
            pltpu.SemaphoreType.DMA((2, 1)),
            pltpu.SemaphoreType.DMA((2, 3)),
            pltpu.SemaphoreType.DMA((2, 3)),
            pltpu.SemaphoreType.DMA((2, 3, RING)),
            pltpu.SemaphoreType.DMA((2, 8)),
            pltpu.SemaphoreType.DMA((1,)),
        ],
        compiler_params=pltpu.CompilerParams(
            collective_id=0, has_side_effects=True, vmem_limit_bytes=56 * 2**20
        ),
        name="key_backward",
    )(residual, key_output_gradient, key_projection_matrix, norm_gain_vector.reshape(1, width))
    devices = lax.axis_size("node") * lax.axis_size("group")
    rows = width // devices
    index = lax.axis_index("node") * lax.axis_size("group") + lax.axis_index("group")
    gain = lax.dynamic_slice(norm_gain_vector, (index * rows,), (rows,))
    scale = float(tokens * devices) ** (-0.5)
    weight_grad = sums[:rows] * (gain * scale)[:, None]
    return (residual_gradient, weight_grad)


def solution(mesh):
    return jax.shard_map(
        on_device,
        mesh=mesh,
        in_specs=(P(("node", "group"), None), P(), P("node", None), P(("node", "group"), None)),
        out_specs=(P(("node", "group"), None), P(("node", "group"), None)),
        check_vma=False,
    )
```

```python
import jax
import jax.numpy as jnp
from jax import lax
from jax.experimental import pallas as pl
from jax.experimental.pallas import tpu as pltpu
from jax.sharding import PartitionSpec as P

MESH = pl.DeviceIdType.MESH
F32, BF16 = jnp.float32, jnp.bfloat16

RING = 4
DEPTH = 16
Z_LO = 8
ORDER = (2, 1, 3, 0)
DIRECT = 128


def place():
    n, g = lax.axis_index("node"), lax.axis_index("group")
    return g // Z_LO, n // 4, (n // 2) % 2 * Z_LO + g % Z_LO, n % 2


def device(x, y, z, c):
    return (y * 4 + z // Z_LO * 2 + c, x * Z_LO + z % Z_LO)


def kernel(
    res_hbm,
    grad_hbm,
    w_hbm,
    gain_ref,
    out_hbm,
    wg_ref,
    res,
    grad,
    both_res,
    both_grad,
    product,
    send1,
    recv1,
    red,
    recv2,
    acc,
    send3,
    recv3,
    w,
    scaled,
    rinv_ref,
    dot_ref,
    out,
    local_sem,
    pair_sem,
    one_sem,
    two_sem,
    three_sem,
    chain_sem,
    wz_sem,
    wa_sem,
    wq_sem,
    wf_sem,
    wb_sem,
    wx_sem,
    wc_sem,
    wd_sem,
    out_sem,
):
    x, y, z, c = place()
    zh = z // Z_LO
    tokens, width = res.shape
    shard = w_hbm.shape[0]
    quarter = shard // RING
    rows = quarter // Z_LO
    first, second = x + c * (y - x), y + c * (x - y)
    other = device(x, y, z, 1 - c)

    def along_first(d):
        return device((x + (1 - c) * d) % RING, (y + c * d) % RING, z, c)

    def along_second(d):
        return device((x + c * d) % RING, (y + (1 - c) * d) % RING, z, c)

    def along_x(d):
        return device((x + d) % RING, y, z, c)

    def along_y(d):
        return device(x, (y + d) % RING, z, c)

    def along_z(d):
        return device(x, y, (z + d) % DEPTH, c)

    def remote(src, dst, sems, index, target):
        return pltpu.make_async_remote_copy(
            src_ref=src,
            dst_ref=dst,
            send_sem=sems.at[(0, *index)],
            recv_sem=sems.at[(1, *index)],
            device_id=target,
            device_id_type=MESH,
        )

    barrier = pltpu.get_barrier_semaphore()
    partners = (
        [along_z(d) for d in (1, 15)]
        + [along_x(d) for d in (1, 2, 3)]
        + [along_y(d) for d in (1, 2, 3)]
        + [other]
    )
    for partner in partners:
        pl.semaphore_signal(barrier, inc=1, device_id=partner, device_id_type=MESH)

    def w_rows(yy, hi, core, count=shard, at=0):
        start = ((yy * 2 + hi) * 2 + core) * shard + at
        return w.at[pl.ds(pl.multiple_of(start, 16), count)]

    def columns(block, core):
        start = block * (2 * shard) + core * 256
        return res_hbm.at[:, pl.ds(pl.multiple_of(start, 128), 384)]

    mine = pl.ds(pl.multiple_of(c * tokens, 16), tokens)
    load_res = pltpu.make_async_copy(res_hbm, res, local_sem.at[0])
    load_grad = pltpu.make_async_copy(grad_hbm, grad, local_sem.at[1])
    load_w = pltpu.make_async_copy(w_hbm, w_rows(y, zh, c), local_sem.at[2])
    load_pair = [
        pltpu.make_async_copy(columns(b, c), both_res.at[b, mine], local_sem.at[3 + b])
        for b in range(8)
    ]
    load_res.start()
    load_grad.start()
    for b in range(8):
        load_pair[b].start()
    load_w.start()
    pl.semaphore_wait(barrier, len(partners))

    swap_grad = remote(both_grad.at[mine], both_grad.at[mine], pair_sem, (8,), other)
    swap_res = [
        remote(columns(b, 1 - c), both_res.at[b, mine], pair_sem, (b,), other) for b in range(8)
    ]
    for b in range(8):
        swap_res[b].start()

    fourth = (shard - DIRECT) // RING

    def w_quarter(yy, xx):
        return w_rows(yy, zh, c, fourth, DIRECT + xx * fourth)

    def w_out(start, count):
        return w_hbm.at[pl.ds(pl.multiple_of(start, 16), count)]

    def w_near_quarter(d):
        return remote(
            w_out(DIRECT + x * fourth, fourth), w_quarter(y, x), wq_sem, (d - 1,), along_y(d)
        )

    def w_near(d):
        return remote(
            w_out(0, DIRECT), w_rows(y, zh, c, DIRECT), wa_sem, (d - 1,), along_y(d)
        )

    def w_fan(d, e):
        piece = w_quarter((y + RING - d) % RING, x)
        return remote(piece, piece, wf_sem, (e - 1, d - 1), along_x(e))

    for d in (2, 1, 3):
        w_near_quarter(d).start()
    for d in (2, 1, 3):
        w_near(d).start()

    def tell(k):
        for d in (1 << k, DEPTH - (1 << k)):
            pl.semaphore_signal(chain_sem.at[k], inc=1, device_id=along_z(d), device_id_type=MESH)

    def hear(k):
        pl.semaphore_wait(chain_sem.at[k], 2)

    tell(0)
    load_grad.wait()
    load_res.wait()

    def square(i, total):
        for k in range(4):
            v = res[:, pl.ds(pl.multiple_of(i * 512 + k * 128, 128), 128)].astype(F32)
            total = total + v * v
        return total

    squares = lax.fori_loop(0, width // 512, square, jnp.zeros((tokens, 128), F32))
    rinv = 1.0 / jnp.sqrt(jnp.sum(squares, axis=1, keepdims=True) / width + 1e-06)
    rinv_ref[...] = jnp.broadcast_to(rinv, (tokens, 128))
    both_grad[mine] = (grad[...].astype(F32) * rinv).astype(BF16)

    swap_grad.start()
    load_w.wait()

    def to_other(yy):
        return remote(w_rows(yy, zh, c), w_rows(yy, zh, c), wc_sem, (yy,), other)

    to_other(y).start()

    for d in (1, 3, 2):
        w_near_quarter(d).wait_recv()
        for e in (2, 1, 3):
            w_fan(d, e).start()

    hear(0)
    tell(1)
    for b in range(8):
        load_pair[b].wait()
    swap_grad.wait_recv()
    for b in range(8):
        swap_res[b].wait_recv()

    def copy_one(d, s):
        return remote(
            send1.at[(first + d) % RING, s], recv1.at[d - 1, s], one_sem, (d - 1, s), along_first(d)
        )

    def partial_block(yy):
        def half(hi, carry):
            product[...] = lax.dot_general(
                both_res[yy * 2 + hi],
                both_grad[...],
                (((0,), (0,)), ((), ())),
                preferred_element_type=F32,
            )
            for q in range(RING):
                at = pl.ds(pl.multiple_of(c * 64 + q * quarter, 16), quarter)
                send1[
                    q + c * (yy - q), yy + c * (q - yy), pl.ds(pl.multiple_of(hi * quarter, 16), quarter)
                ] = product[at].astype(BF16)
            return carry

        lax.fori_loop(0, 2, half, 0)

    for step in ORDER:
        yy = (y + step) % RING
        partial_block(yy)
        if step == 3:
            hear(1)
            tell(2)

        @pl.when(c == 0)
        def _(yy=yy):
            for d in (2, 1, 3):
                copy_one(d, yy).start()

    @pl.when(c == 1)
    def _():
        for step in ORDER:
            for d in (2, 1, 3):
                copy_one(d, (x + step) % RING).start()

    w_far = remote(
        w_out(x * quarter, quarter), w_rows(y, zh, c, quarter, x * quarter), wz_sem, (0,), along_z(8)
    )
    hear(2)
    w_far.start()

    lo = 1 - zh

    def w_piece(core, yy, xx):
        return w_rows(yy, lo, core, quarter, xx * quarter)

    def w_side(d):
        return remote(w_piece(c, y, x), w_piece(c, y, x), wb_sem, (d - 1,), along_second(d))

    def copy_two(e):
        return remote(red.at[(second + e) % RING], recv2.at[e - 1], two_sem, (e - 1,), along_second(e))

    for step in ORDER:
        s = (second + step) % RING
        for d in (1, 2, 3):
            copy_one(d, s).wait_recv()

        def add(i, carry, s=s, step=step):
            at = pl.ds(pl.multiple_of(i * 16, 16), 16)
            total = send1[first, s, at].astype(F32)
            for k in range(3):
                total = total + recv1[k, s, at].astype(F32)
            if step:
                red[s, at] = total.astype(BF16)
            else:
                acc[at] = total
            return carry

        lax.fori_loop(0, 2 * quarter // 16, add, 0)
        if step:
            copy_two(step).start()

    def piece_of(k, back=0):
        xx, yy = (x + RING - back) % RING, (y + RING - back) % RING
        return k + c * (yy - k), xx + c * (k - xx)

    def w_across(d, k):
        piece = w_piece(c, *piece_of(k))
        return remote(piece, piece, wx_sem, (d - 1, k), along_first(d))

    def w_far_other(yy, xx):
        piece = w_piece(c, yy, xx)
        return remote(piece, piece, wd_sem, (yy, xx), other)

    w_far.wait_recv()
    for d in (2, 1, 3):
        w_side(d).start()

    dot_ref[...] = jnp.zeros_like(dot_ref)

    def features(block):
        at = pl.ds(pl.multiple_of(block * (2 * shard), 128), 2 * shard)
        value = lax.dot_general(
            grad[...],
            w[pl.ds(pl.multiple_of(block * (2 * shard), 16), 2 * shard)],
            (((1,), (1,)), ((), ())),
            preferred_element_type=F32,
        )
        value = value * gain_ref[:, at]
        scaled[:, at] = value
        value = value * res[:, at].astype(F32)
        part = dot_ref[...]
        for k in range(2 * shard // 128):
            part = part + value[:, k * 128 : (k + 1) * 128]
        dot_ref[...] = part

    def from_other(yy):
        piece = w_rows(yy, zh, 1 - c)
        remote(piece, piece, wc_sem, (yy,), other).wait_recv()

    for d in (1, 3, 2):
        w_near(d).wait_recv()
        for e in (1, 2, 3):
            piece = w_quarter((y + RING - d) % RING, (x + RING - e) % RING)
            remote(piece, piece, wf_sem, (e - 1, d - 1), along_x(e)).wait_recv()
        to_other((y + RING - d) % RING).start()
    for d in (0, 1, 3, 2):
        yy = (y + RING - d) % RING
        from_other(yy)
        features(yy * 2 + zh)

    for e in (1, 3, 2):
        copy_two(e).wait_recv()

    def add_two(i, carry):
        at = pl.ds(pl.multiple_of(i * 16, 16), 16)
        total = acc[at]
        for k in range(3):
            total = total + recv2[k, at].astype(F32)
        acc[at] = total
        return carry

    lax.fori_loop(0, 2 * quarter // 16, add_two, 0)
    acc[2 * quarter :] = jnp.zeros((acc.shape[0] - 2 * quarter, acc.shape[1]), F32)
    for k in range(DEPTH):
        send3[k] = acc[k * rows : k * rows + 16].astype(BF16)

    def copy_three(d):
        return remote(send3.at[(z + d) % DEPTH], recv3.at[d - 1], three_sem, (d - 1,), along_z(d))

    distances = (8, 7, 9, 6, 10, 5, 11, 4, 12, 3, 13, 2, 14, 1, 15)
    for d in distances:
        copy_three(d).start()

    for d in (1, 2, 3):
        w_side(d).wait_recv()
    for k in range(RING):
        for d in (2, 1, 3):
            w_across(d, k).start()
    for k in range(RING):
        w_far_other(*piece_of(k)).start()

    for k in range(RING):
        for d in (1, 3, 2):
            piece = w_piece(c, *piece_of(k, d))
            remote(piece, piece, wx_sem, (d - 1, k), along_first(d)).wait_recv()
            w_far_other(*piece_of(k, d)).start()
    for yy in range(RING):
        for xx in range(RING):
            piece = w_piece(1 - c, yy, xx)
            remote(piece, piece, wd_sem, (yy, xx), other).wait_recv()
        features(yy * 2 + lo)

    def finish(i, carry):
        at = pl.ds(pl.multiple_of(i * 16, 16), 16)
        rinv = rinv_ref[at][:, :1]
        factor = jnp.sum(dot_ref[at], axis=1, keepdims=True) * (1.0 / width) * rinv * rinv
        out[at] = ((scaled[at] - res[at].astype(F32) * factor) * rinv).astype(BF16)
        return carry

    stores = []
    for k in range(4):
        part = pl.ds(k * (tokens // 4), tokens // 4)
        lax.fori_loop(k * (tokens // 64), (k + 1) * (tokens // 64), finish, 0)
        stores.append(pltpu.make_async_copy(out.at[part], out_hbm.at[part], out_sem.at[k]))
        stores[-1].start()

    place_of_rows = (lax.axis_index("node") * (RING * Z_LO) + lax.axis_index("group")) * rows
    lane = lax.broadcasted_iota(jnp.int32, (16, width), 1)
    row = lax.broadcasted_iota(jnp.int32, (16, width), 0)
    own_gain = jnp.sum(
        jnp.where(lane == row + place_of_rows, gain_ref[...], 0.0), axis=1, keepdims=True
    )
    scale = float(tokens * RING * RING * DEPTH * 2) ** (-0.5)

    for d in distances:
        copy_three(d).wait_recv()
    total = send3[z].astype(F32)
    for k in range(DEPTH - 1):
        total = total + recv3[k].astype(F32)
    wg_ref[...] = (total * (own_gain * scale))[:rows]

    swap_grad.wait_send()
    for b in range(8):
        swap_res[b].wait_send()
    w_far.wait_send()
    for d in (1, 2, 3):
        w_near(d).wait_send()
        w_near_quarter(d).wait_send()
        w_side(d).wait_send()
        copy_two(d).wait_send()
        for e in (1, 2, 3):
            w_fan(d, e).wait_send()
        for s in range(RING):
            copy_one(d, s).wait_send()
            w_across(d, s).wait_send()
    for yy in range(RING):
        to_other(yy).wait_send()
        for d in range(RING):
            w_far_other(*piece_of(yy, d)).wait_send()
    for d in distances:
        copy_three(d).wait_send()
    for store in stores:
        store.wait()


def on_device(residual, norm_gain_vector, key_projection_matrix, key_output_gradient):
    tokens, width = residual.shape
    features = key_output_gradient.shape[1]
    shard = key_projection_matrix.shape[0]
    quarter = shard // RING
    hbm = pl.BlockSpec(memory_space=pltpu.HBM)
    vmem = pl.BlockSpec(memory_space=pltpu.VMEM)
    return pl.pallas_call(
        kernel,
        out_shape=(
            pltpu.VMEM((tokens, width), BF16),
            pltpu.VMEM((shard // (RING * Z_LO), features), F32),
        ),
        in_specs=[hbm, hbm, hbm, vmem],
        out_specs=(pl.BlockSpec(memory_space=pl.ANY), vmem),
        scratch_shapes=[
            pltpu.VMEM((tokens, width), BF16),
            pltpu.VMEM((tokens, features), BF16),
            pltpu.VMEM((8, 2 * tokens, 384), BF16),
            pltpu.VMEM((2 * tokens, features), BF16),
            pltpu.VMEM((384, features), F32),
            pltpu.VMEM((RING, RING, 2 * quarter, features), BF16),
            pltpu.VMEM((3, RING, 2 * quarter, features), BF16),
            pltpu.VMEM((RING, 2 * quarter, features), BF16),
            pltpu.VMEM((3, 2 * quarter, features), BF16),
            pltpu.VMEM((2 * quarter + 16, features), F32),
            pltpu.VMEM((DEPTH, 16, features), BF16),
            pltpu.VMEM((DEPTH - 1, 16, features), BF16),
            pltpu.VMEM((width, features), BF16),
            pltpu.VMEM((tokens, width), F32),
            pltpu.VMEM((tokens, 128), F32),
            pltpu.VMEM((tokens, 128), F32),
            pltpu.VMEM((tokens, width), BF16),
            pltpu.SemaphoreType.DMA((11,)),
            pltpu.SemaphoreType.DMA((2, 9)),
            pltpu.SemaphoreType.DMA((2, 3, RING)),
            pltpu.SemaphoreType.DMA((2, 3)),
            pltpu.SemaphoreType.DMA((2, DEPTH - 1)),
            pltpu.SemaphoreType.REGULAR((3,)),
            pltpu.SemaphoreType.DMA((2, 1)),
            pltpu.SemaphoreType.DMA((2, 3)),
            pltpu.SemaphoreType.DMA((2, 3)),
            pltpu.SemaphoreType.DMA((2, 3, 3)),
            pltpu.SemaphoreType.DMA((2, 3)),
            pltpu.SemaphoreType.DMA((2, 3, RING)),
            pltpu.SemaphoreType.DMA((2, RING)),
            pltpu.SemaphoreType.DMA((2, RING, RING)),
            pltpu.SemaphoreType.DMA((4,)),
        ],
        compiler_params=pltpu.CompilerParams(
            collective_id=0, has_side_effects=True, vmem_limit_bytes=54 * 2**20
        ),
        name="key_backward",
    )(residual, key_output_gradient, key_projection_matrix, norm_gain_vector.reshape(1, width))


def solution(mesh):
    return jax.shard_map(
        on_device,
        mesh=mesh,
        in_specs=(P(("node", "group"), None), P(), P("node", None), P(("node", "group"), None)),
        out_specs=(P(("node", "group"), None), P(("node", "group"), None)),
        check_vma=False,
    )
```

```python
import jax
import jax.numpy as jnp
from jax import lax
from jax.experimental import pallas as pl
from jax.experimental.pallas import tpu as pltpu
from jax.sharding import PartitionSpec as P

MESH = pl.DeviceIdType.MESH
F32, BF16 = jnp.float32, jnp.bfloat16

RING = 4
DEPTH = 16
Z_LO = 8
ORDER = (2, 1, 3, 0)
REACH = 4


def place():
    n, g = lax.axis_index("node"), lax.axis_index("group")
    return g // Z_LO, n // 4, (n // 2) % 2 * Z_LO + g % Z_LO, n % 2


def device(x, y, z, c):
    return (y * 4 + z // Z_LO * 2 + c, x * Z_LO + z % Z_LO)


def kernel(
    res_hbm,
    grad_hbm,
    w_hbm,
    gain_ref,
    out_hbm,
    wg_ref,
    res,
    grad,
    both_res,
    both_grad,
    product,
    send1,
    recv1,
    red,
    recv2,
    acc,
    send3,
    recv3,
    w,
    scaled,
    rinv_ref,
    dot_ref,
    out,
    local_sem,
    pair_sem,
    one_sem,
    two_sem,
    three_sem,
    chain_sem,
    wz_sem,
    wa_sem,
    ws_sem,
    wb_sem,
    wx_sem,
    wc_sem,
    wd_sem,
    out_sem,
):
    x, y, z, c = place()
    zh = z // Z_LO
    tokens, width = res.shape
    shard = w_hbm.shape[0]
    quarter = shard // RING
    rows = quarter // Z_LO
    first, second = x + c * (y - x), y + c * (x - y)
    other = device(x, y, z, 1 - c)

    def along_first(d):
        return device((x + (1 - c) * d) % RING, (y + c * d) % RING, z, c)

    def along_second(d):
        return device((x + c * d) % RING, (y + (1 - c) * d) % RING, z, c)

    def along_x(d):
        return device((x + d) % RING, y, z, c)

    def along_y(d):
        return device(x, (y + d) % RING, z, c)

    def along_z(d):
        return device(x, y, (z + d) % DEPTH, c)

    def remote(src, dst, sems, index, target):
        return pltpu.make_async_remote_copy(
            src_ref=src,
            dst_ref=dst,
            send_sem=sems.at[(0, *index)],
            recv_sem=sems.at[(1, *index)],
            device_id=target,
            device_id_type=MESH,
        )

    barrier = pltpu.get_barrier_semaphore()
    partners = (
        [along_z(d) for d in (1, 15)]
        + [along_x(d) for d in (1, 2, 3)]
        + [along_y(d) for d in (1, 2, 3)]
        + [other]
    )
    for partner in partners:
        pl.semaphore_signal(barrier, inc=1, device_id=partner, device_id_type=MESH)

    def w_rows(yy, hi, core, count=shard, at=0):
        start = ((yy * 2 + hi) * 2 + core) * shard + at
        return w.at[pl.ds(pl.multiple_of(start, 16), count)]

    def columns(block, core):
        start = block * (2 * shard) + core * 256
        return res_hbm.at[:, pl.ds(pl.multiple_of(start, 128), 384)]

    mine = pl.ds(pl.multiple_of(c * tokens, 16), tokens)
    load_res = pltpu.make_async_copy(res_hbm, res, local_sem.at[0])
    load_grad = pltpu.make_async_copy(grad_hbm, grad, local_sem.at[1])
    load_w = pltpu.make_async_copy(w_hbm, w_rows(y, zh, c), local_sem.at[2])
    load_pair = [
        pltpu.make_async_copy(columns(b, c), both_res.at[b, mine], local_sem.at[3 + b])
        for b in range(8)
    ]
    load_res.start()
    load_grad.start()
    for b in range(8):
        load_pair[b].start()
    load_w.start()
    pl.semaphore_wait(barrier, len(partners))

    swap_grad = remote(both_grad.at[mine], both_grad.at[mine], pair_sem, (8,), other)
    swap_res = [
        remote(columns(b, 1 - c), both_res.at[b, mine], pair_sem, (b,), other) for b in range(8)
    ]
    for b in range(8):
        swap_res[b].start()

    half_shard = shard // 2
    parity = z % 2

    def w_out(start, count):
        return w_hbm.at[pl.ds(pl.multiple_of(start, 16), count)]

    def w_near(d):
        return remote(
            w_out(parity * half_shard, half_shard),
            w_rows(y, zh, c, half_shard, parity * half_shard),
            wa_sem,
            (d - 1,),
            along_y(d),
        )

    def w_swap(d):
        piece = w_rows((y + RING - d) % RING, zh, c, half_shard, parity * half_shard)
        return remote(piece, piece, ws_sem, (d - 1,), device(x, y, z + 1 - 2 * parity, c))

    for d in (2, 1, 3):
        w_near(d).start()

    def tell(k):
        for d in (1 << k, DEPTH - (1 << k)):
            pl.semaphore_signal(chain_sem.at[k], inc=1, device_id=along_z(d), device_id_type=MESH)

    def hear(k):
        pl.semaphore_wait(chain_sem.at[k], 2)

    tell(0)
    load_grad.wait()
    load_res.wait()

    def square(i, total):
        for k in range(4):
            v = res[:, pl.ds(pl.multiple_of(i * 512 + k * 128, 128), 128)].astype(F32)
            total = total + v * v
        return total

    squares = lax.fori_loop(0, width // 512, square, jnp.zeros((tokens, 128), F32))
    rinv = 1.0 / jnp.sqrt(jnp.sum(squares, axis=1, keepdims=True) / width + 1e-06)
    rinv_ref[...] = jnp.broadcast_to(rinv, (tokens, 128))
    both_grad[mine] = (grad[...].astype(F32) * rinv).astype(BF16)

    swap_grad.start()
    load_w.wait()

    def to_other(yy):
        return remote(w_rows(yy, zh, c), w_rows(yy, zh, c), wc_sem, (yy,), other)

    to_other(y).start()

    hear(0)
    tell(1)
    for b in range(8):
        load_pair[b].wait()
    swap_grad.wait_recv()
    for b in range(8):
        swap_res[b].wait_recv()

    def copy_one(d, s):
        return remote(
            send1.at[(first + d) % RING, s], recv1.at[d - 1, s], one_sem, (d - 1, s), along_first(d)
        )

    def partial_block(yy):
        def half(hi, carry):
            product[...] = lax.dot_general(
                both_res[yy * 2 + hi],
                both_grad[...],
                (((0,), (0,)), ((), ())),
                preferred_element_type=F32,
            )
            for q in range(RING):
                at = pl.ds(pl.multiple_of(c * 64 + q * quarter, 16), quarter)
                send1[
                    q + c * (yy - q), yy + c * (q - yy), pl.ds(pl.multiple_of(hi * quarter, 16), quarter)
                ] = product[at].astype(BF16)
            return carry

        lax.fori_loop(0, 2, half, 0)

    z_lo = z % Z_LO
    sends_far = (z_lo == 0) | (z_lo == Z_LO - 1)

    def w_far(j):
        target = (z + DEPTH + jnp.where(z_lo == 0, -1 - j, 1 + j)) % DEPTH
        return pltpu.make_async_remote_copy(
            src_ref=w_out(x * quarter, quarter),
            dst_ref=w_rows(y, zh, c, quarter, x * quarter),
            send_sem=wz_sem.at[0, j],
            recv_sem=wz_sem.at[1, 0],
            device_id=device(x, y, target, c),
            device_id_type=MESH,
        )

    for step in ORDER:
        yy = (y + step) % RING
        partial_block(yy)
        if step == 1:
            hear(1)
            tell(2)

            @pl.when(sends_far)
            def _():
                for j in range(REACH - 1, -1, -1):
                    w_far(j).start()

        @pl.when(c == 0)
        def _(yy=yy):
            for d in (2, 1, 3):
                copy_one(d, yy).start()

    @pl.when(c == 1)
    def _():
        for step in ORDER:
            for d in (2, 1, 3):
                copy_one(d, (x + step) % RING).start()

    for d in (1, 3, 2):
        w_near(d).wait_recv()
        w_swap(d).start()

    lo = 1 - zh

    def w_piece(core, yy, xx):
        return w_rows(yy, lo, core, quarter, xx * quarter)

    def w_side(d):
        return remote(w_piece(c, y, x), w_piece(c, y, x), wb_sem, (d - 1,), along_second(d))

    def copy_two(e):
        return remote(red.at[(second + e) % RING], recv2.at[e - 1], two_sem, (e - 1,), along_second(e))

    for step in ORDER:
        s = (second + step) % RING
        for d in (1, 2, 3):
            copy_one(d, s).wait_recv()

        def add(i, carry, s=s, step=step):
            at = pl.ds(pl.multiple_of(i * 16, 16), 16)
            total = send1[first, s, at].astype(F32)
            for k in range(3):
                total = total + recv1[k, s, at].astype(F32)
            if step:
                red[s, at] = total.astype(BF16)
            else:
                acc[at] = total
            return carry

        lax.fori_loop(0, 2 * quarter // 16, add, 0)
        if step:
            copy_two(step).start()
        if step == 1:
            w_far(0).wait_recv()
            for d in (2, 1, 3):
                w_side(d).start()

    def w_across(d, yy):
        piece = w_piece(0, yy, x)
        return remote(piece, piece, wx_sem, (d - 1, yy), along_x(d))

    def w_whole(d):
        piece = w_rows(y, lo, 1)
        return remote(piece, piece, wx_sem, (d - 1, 0), along_y(d))

    def to_other_far(yy):
        return remote(w_rows(yy, lo, c), w_rows(yy, lo, c), wd_sem, (yy,), other)

    for d in (1, 3, 2):
        w_swap(d).wait_recv()
        to_other((y + RING - d) % RING).start()
    for d in (1, 2, 3):
        w_side(d).wait_recv()

    @pl.when(c == 0)
    def _():
        for back in (0, 1, 3, 2):
            for d in (2, 1, 3):
                w_across(d, (y + RING - back) % RING).start()

    @pl.when(c == 1)
    def _():
        for d in (1, 3, 2):
            w_whole(d).start()

    dot_ref[...] = jnp.zeros_like(dot_ref)

    def features(block):
        at = pl.ds(pl.multiple_of(block * (2 * shard), 128), 2 * shard)
        value = lax.dot_general(
            grad[...],
            w[pl.ds(pl.multiple_of(block * (2 * shard), 16), 2 * shard)],
            (((1,), (1,)), ((), ())),
            preferred_element_type=F32,
        )
        value = value * gain_ref[:, at]
        scaled[:, at] = value
        value = value * res[:, at].astype(F32)
        part = dot_ref[...]
        for k in range(2 * shard // 128):
            part = part + value[:, k * 128 : (k + 1) * 128]
        dot_ref[...] = part

    def from_other(yy):
        piece = w_rows(yy, zh, 1 - c)
        remote(piece, piece, wc_sem, (yy,), other).wait_recv()

    for d in (0, 1, 3, 2):
        yy = (y + RING - d) % RING
        from_other(yy)
        features(yy * 2 + zh)

    for e in (1, 3, 2):
        copy_two(e).wait_recv()

    def add_two(i, carry):
        at = pl.ds(pl.multiple_of(i * 16, 16), 16)
        total = acc[at]
        for k in range(3):
            total = total + recv2[k, at].astype(F32)
        acc[at] = total
        return carry

    lax.fori_loop(0, 2 * quarter // 16, add_two, 0)
    acc[2 * quarter :] = jnp.zeros((acc.shape[0] - 2 * quarter, acc.shape[1]), F32)
    for k in range(DEPTH):
        send3[k] = acc[k * rows : k * rows + 16].astype(BF16)

    def copy_three(d):
        return remote(send3.at[(z + d) % DEPTH], recv3.at[d - 1], three_sem, (d - 1,), along_z(d))

    hear(2)
    distances = (8, 7, 9, 6, 10, 5, 11, 4, 12, 3, 13, 2, 14, 1, 15)
    for d in distances:
        copy_three(d).start()

    def from_other_far(yy):
        piece = w_rows(yy, lo, 1 - c)
        remote(piece, piece, wd_sem, (yy,), other).wait_recv()
        features(yy * 2 + lo)

    before = None
    for back in (0, 1, 3, 2):
        yy = (y + RING - back) % RING

        @pl.when(c == 0)
        def _(yy=yy):
            for d in (1, 3, 2):
                piece = w_piece(0, yy, (x + RING - d) % RING)
                remote(piece, piece, wx_sem, (d - 1, yy), along_x(d)).wait_recv()

        if back:

            @pl.when(c == 1)
            def _(yy=yy, back=back):
                piece = w_rows(yy, lo, 1)
                remote(piece, piece, wx_sem, (back - 1, 0), along_y(back)).wait_recv()

        to_other_far(yy).start()
        if before is not None:
            from_other_far(before)
        before = yy
    from_other_far(before)

    def finish(i, carry):
        at = pl.ds(pl.multiple_of(i * 16, 16), 16)
        rinv = rinv_ref[at][:, :1]
        factor = jnp.sum(dot_ref[at], axis=1, keepdims=True) * (1.0 / width) * rinv * rinv
        out[at] = ((scaled[at] - res[at].astype(F32) * factor) * rinv).astype(BF16)
        return carry

    stores = []
    for k in range(4):
        part = pl.ds(k * (tokens // 4), tokens // 4)
        lax.fori_loop(k * (tokens // 64), (k + 1) * (tokens // 64), finish, 0)
        stores.append(pltpu.make_async_copy(out.at[part], out_hbm.at[part], out_sem.at[k]))
        stores[-1].start()

    place_of_rows = (lax.axis_index("node") * (RING * Z_LO) + lax.axis_index("group")) * rows
    lane = lax.broadcasted_iota(jnp.int32, (16, width), 1)
    row = lax.broadcasted_iota(jnp.int32, (16, width), 0)
    own_gain = jnp.sum(
        jnp.where(lane == row + place_of_rows, gain_ref[...], 0.0), axis=1, keepdims=True
    )
    scale = float(tokens * RING * RING * DEPTH * 2) ** (-0.5)

    for d in distances:
        copy_three(d).wait_recv()
    total = send3[z].astype(F32)
    for k in range(DEPTH - 1):
        total = total + recv3[k].astype(F32)
    wg_ref[...] = (total * (own_gain * scale))[:rows]

    swap_grad.wait_send()
    for b in range(8):
        swap_res[b].wait_send()
    @pl.when(sends_far)
    def _():
        for j in range(REACH):
            w_far(j).wait_send()

    for d in (1, 2, 3):
        w_near(d).wait_send()
        w_swap(d).wait_send()
        w_side(d).wait_send()
        copy_two(d).wait_send()
        for s in range(RING):
            copy_one(d, s).wait_send()

    @pl.when(c == 0)
    def _():
        for d in (1, 2, 3):
            for yy in range(RING):
                w_across(d, yy).wait_send()

    @pl.when(c == 1)
    def _():
        for d in (1, 2, 3):
            w_whole(d).wait_send()

    for yy in range(RING):
        to_other(yy).wait_send()
        to_other_far(yy).wait_send()
    for d in distances:
        copy_three(d).wait_send()
    for store in stores:
        store.wait()


def on_device(residual, norm_gain_vector, key_projection_matrix, key_output_gradient):
    tokens, width = residual.shape
    features = key_output_gradient.shape[1]
    shard = key_projection_matrix.shape[0]
    quarter = shard // RING
    hbm = pl.BlockSpec(memory_space=pltpu.HBM)
    vmem = pl.BlockSpec(memory_space=pltpu.VMEM)
    return pl.pallas_call(
        kernel,
        out_shape=(
            pltpu.VMEM((tokens, width), BF16),
            pltpu.VMEM((shard // (RING * Z_LO), features), F32),
        ),
        in_specs=[hbm, hbm, hbm, vmem],
        out_specs=(pl.BlockSpec(memory_space=pl.ANY), vmem),
        scratch_shapes=[
            pltpu.VMEM((tokens, width), BF16),
            pltpu.VMEM((tokens, features), BF16),
            pltpu.VMEM((8, 2 * tokens, 384), BF16),
            pltpu.VMEM((2 * tokens, features), BF16),
            pltpu.VMEM((384, features), F32),
            pltpu.VMEM((RING, RING, 2 * quarter, features), BF16),
            pltpu.VMEM((3, RING, 2 * quarter, features), BF16),
            pltpu.VMEM((RING, 2 * quarter, features), BF16),
            pltpu.VMEM((3, 2 * quarter, features), BF16),
            pltpu.VMEM((2 * quarter + 16, features), F32),
            pltpu.VMEM((DEPTH, 16, features), BF16),
            pltpu.VMEM((DEPTH - 1, 16, features), BF16),
            pltpu.VMEM((width, features), BF16),
            pltpu.VMEM((tokens, width), F32),
            pltpu.VMEM((tokens, 128), F32),
            pltpu.VMEM((tokens, 128), F32),
            pltpu.VMEM((tokens, width), BF16),
            pltpu.SemaphoreType.DMA((11,)),
            pltpu.SemaphoreType.DMA((2, 9)),
            pltpu.SemaphoreType.DMA((2, 3, RING)),
            pltpu.SemaphoreType.DMA((2, 3)),
            pltpu.SemaphoreType.DMA((2, DEPTH - 1)),
            pltpu.SemaphoreType.REGULAR((3,)),
            pltpu.SemaphoreType.DMA((2, REACH)),
            pltpu.SemaphoreType.DMA((2, 3)),
            pltpu.SemaphoreType.DMA((2, 3)),
            pltpu.SemaphoreType.DMA((2, 3)),
            pltpu.SemaphoreType.DMA((2, 3, RING)),
            pltpu.SemaphoreType.DMA((2, RING)),
            pltpu.SemaphoreType.DMA((2, RING)),
            pltpu.SemaphoreType.DMA((4,)),
        ],
        compiler_params=pltpu.CompilerParams(
            collective_id=0, has_side_effects=True, vmem_limit_bytes=54 * 2**20
        ),
        name="key_backward",
    )(residual, key_output_gradient, key_projection_matrix, norm_gain_vector.reshape(1, width))


def solution(mesh):
    return jax.shard_map(
        on_device,
        mesh=mesh,
        in_specs=(P(("node", "group"), None), P(), P("node", None), P(("node", "group"), None)),
        out_specs=(P(("node", "group"), None), P(("node", "group"), None)),
        check_vma=False,
    )
```

```python
import jax
import jax.numpy as jnp
from jax import lax
from jax.experimental import pallas as pl
from jax.experimental.pallas import tpu as pltpu
from jax.sharding import PartitionSpec as P

MESH = pl.DeviceIdType.MESH
F32, BF16 = jnp.float32, jnp.bfloat16

RING = 4
DEPTH = 16
Z_LO = 8
BLOCK = 128
ORDER = (2, 1, 3, 0)
REACH = 4


def place():
    n, g = lax.axis_index("node"), lax.axis_index("group")
    return g // Z_LO, n // 4, (n // 2) % 2 * Z_LO + g % Z_LO, n % 2


def device(x, y, z, c):
    return (y * 4 + z // Z_LO * 2 + c, x * Z_LO + z % Z_LO)


def kernel(
    res_hbm,
    grad_hbm,
    w_hbm,
    gain_ref,
    out,
    wg_ref,
    res,
    grad,
    both_res,
    both_grad,
    turned,
    send1,
    recv1,
    red,
    recv2,
    acc,
    packed,
    send3,
    recv3,
    w,
    scaled,
    rinv_ref,
    dot_ref,
    local_sem,
    pair_sem,
    one_sem,
    two_sem,
    three_sem,
    chain_sem,
    wz_sem,
    wa_sem,
    ws_sem,
    wb_sem,
    wx_sem,
    wc_sem,
    wd_sem,
):
    x, y, z, c = place()
    zh = z // Z_LO
    tokens, width = res.shape
    shard = w_hbm.shape[0]
    quarter = shard // RING
    rows = quarter // Z_LO
    first, second = x + c * (y - x), y + c * (x - y)
    other = device(x, y, z, 1 - c)

    def along_first(d):
        return device((x + (1 - c) * d) % RING, (y + c * d) % RING, z, c)

    def along_second(d):
        return device((x + c * d) % RING, (y + (1 - c) * d) % RING, z, c)

    def along_x(d):
        return device((x + d) % RING, y, z, c)

    def along_y(d):
        return device(x, (y + d) % RING, z, c)

    def along_z(d):
        return device(x, y, (z + d) % DEPTH, c)

    def remote(src, dst, sems, index, target):
        return pltpu.make_async_remote_copy(
            src_ref=src,
            dst_ref=dst,
            send_sem=sems.at[(0, *index)],
            recv_sem=sems.at[(1, *index)],
            device_id=target,
            device_id_type=MESH,
        )

    barrier = pltpu.get_barrier_semaphore()
    partners = (
        [along_z(d) for d in (1, 15)]
        + [along_x(d) for d in (1, 2, 3)]
        + [along_y(d) for d in (1, 2, 3)]
        + [other]
    )
    for partner in partners:
        pl.semaphore_signal(barrier, inc=1, device_id=partner, device_id_type=MESH)

    def w_rows(yy, hi, core, count=shard, at=0):
        start = ((yy * 2 + hi) * 2 + core) * shard + at
        return w.at[pl.ds(pl.multiple_of(start, 16), count)]

    def columns(block, core):
        start = block * (2 * shard) + core * 256
        return res_hbm.at[:, pl.ds(pl.multiple_of(start, 128), 384)]

    mine = pl.ds(pl.multiple_of(c * tokens, 16), tokens)
    load_res = pltpu.make_async_copy(res_hbm, res, local_sem.at[0])
    load_grad = pltpu.make_async_copy(grad_hbm, grad, local_sem.at[1])
    load_w = pltpu.make_async_copy(w_hbm, w_rows(y, zh, c), local_sem.at[2])

    def load_pair(b):
        return pltpu.make_async_copy(columns(b, c), both_res.at[b, mine], local_sem.at[3 + b])

    load_res.start()
    load_grad.start()
    for b in range(8):
        load_pair(b).start()
    load_w.start()
    pl.semaphore_wait(barrier, len(partners))

    swap_grad = remote(both_grad.at[mine], both_grad.at[mine], pair_sem, (8,), other)

    def swap_res(b):
        return remote(columns(b, 1 - c), both_res.at[b, mine], pair_sem, (b,), other)

    for b in range(8):
        swap_res(b).start()

    half_shard = shard // 2
    parity = z % 2

    def w_out(start, count):
        return w_hbm.at[pl.ds(pl.multiple_of(start, 16), count)]

    def w_near(d):
        return remote(
            w_out(parity * half_shard, half_shard),
            w_rows(y, zh, c, half_shard, parity * half_shard),
            wa_sem,
            (d - 1,),
            along_y(d),
        )

    def w_swap(d):
        piece = w_rows((y + RING - d) % RING, zh, c, half_shard, parity * half_shard)
        return remote(piece, piece, ws_sem, (d - 1,), device(x, y, z + 1 - 2 * parity, c))

    for d in (2, 1, 3):
        w_near(d).start()

    def tell(k):
        for d in (1 << k, DEPTH - (1 << k)):
            pl.semaphore_signal(chain_sem.at[k], inc=1, device_id=along_z(d), device_id_type=MESH)

    def hear(k):
        pl.semaphore_wait(chain_sem.at[k], 2)

    tell(0)
    load_grad.wait()
    load_res.wait()
    hear(0)
    tell(1)

    def square(i, total):
        for k in range(4):
            v = res[:, pl.ds(pl.multiple_of(i * 512 + k * 128, 128), 128)].astype(F32)
            total = total + v * v
        return total

    squares = lax.fori_loop(0, width // 512, square, jnp.zeros((tokens, 128), F32))
    rinv = 1.0 / jnp.sqrt(jnp.sum(squares, axis=1, keepdims=True) / width + 1e-06)
    rinv_ref[...] = jnp.broadcast_to(rinv, (tokens, 128))
    both_grad[mine] = (grad[...].astype(F32) * rinv).astype(BF16)

    swap_grad.start()
    load_w.wait()

    def to_other(yy):
        return remote(w_rows(yy, zh, c), w_rows(yy, zh, c), wc_sem, (yy,), other)

    to_other(y).start()

    z_lo = z % Z_LO
    sends_far = (z_lo == 0) | (z_lo == Z_LO - 1)

    def w_far(j):
        target = (z + DEPTH + jnp.where(z_lo == 0, -1 - j, 1 + j)) % DEPTH
        return pltpu.make_async_remote_copy(
            src_ref=w_out(x * quarter, quarter),
            dst_ref=w_rows(y, zh, c, quarter, x * quarter),
            send_sem=wz_sem.at[0, j],
            recv_sem=wz_sem.at[1, 0],
            device_id=device(x, y, target, c),
            device_id_type=MESH,
        )

    hear(1)

    @pl.when(sends_far)
    def _():
        for j in range(REACH - 1, -1, -1):
            w_far(j).start()

    tell(2)

    def turn(b, carry):
        load_pair(b).wait()
        swap_res(b).wait_recv()
        turned[b] = both_res[b].T
        return carry

    lax.fori_loop(0, 8, turn, 0)
    swap_grad.wait_recv()

    def copy_one(d, s):
        return remote(
            send1.at[(first + d) % RING, s], recv1.at[d - 1, s], one_sem, (d - 1, s), along_first(d)
        )

    def partial_block(yy):
        def half(hi, carry):
            value = jnp.dot(
                turned[yy * 2 + hi, pl.ds(pl.multiple_of(c * 64, 64), shard)],
                both_grad[...],
                preferred_element_type=F32,
            ).astype(BF16)
            for q in range(RING):
                send1[
                    q + c * (yy - q), yy + c * (q - yy), pl.ds(pl.multiple_of(hi * quarter, 16), quarter)
                ] = value[q * quarter : (q + 1) * quarter]
            return carry

        lax.fori_loop(0, 2, half, 0)

    for step in ORDER:
        yy = (y + step) % RING
        partial_block(yy)

        @pl.when(c == 0)
        def _(yy=yy):
            for d in (2, 1, 3):
                copy_one(d, yy).start()

    @pl.when(c == 1)
    def _():
        for step in ORDER:
            for d in (2, 1, 3):
                copy_one(d, (x + step) % RING).start()

    for d in (1, 3, 2):
        w_near(d).wait_recv()
        w_swap(d).start()

    lo = 1 - zh

    def w_piece(core, yy, xx):
        return w_rows(yy, lo, core, quarter, xx * quarter)

    def w_side(d):
        return remote(w_piece(c, y, x), w_piece(c, y, x), wb_sem, (d - 1,), along_second(d))

    def copy_two(e):
        return remote(red.at[(second + e) % RING], recv2.at[e - 1], two_sem, (e - 1,), along_second(e))

    def w_across(d, yy):
        piece = w_piece(0, yy, x)
        return remote(piece, piece, wx_sem, (d - 1, yy), along_x(d))

    def w_whole(d):
        piece = w_rows(y, lo, 1)
        return remote(piece, piece, wx_sem, (d - 1, 0), along_y(d))

    def to_other_far(yy):
        return remote(w_rows(yy, lo, c), w_rows(yy, lo, c), wd_sem, (yy,), other)

    def first_part():
        w_far(0).wait_recv()
        for d in (2, 1, 3):
            w_side(d).start()

    def second_part():
        for d in (1, 2, 3):
            w_side(d).wait_recv()

        @pl.when(c == 0)
        def _():
            for back in (0, 1, 3, 2):
                for d in (2, 1, 3):
                    w_across(d, (y + RING - back) % RING).start()

        @pl.when(c == 1)
        def _():
            for d in (1, 3, 2):
                w_whole(d).start()

    for step in ORDER:
        s = (second + step) % RING
        for d in (1, 2, 3):
            copy_one(d, s).wait_recv()

        def add(i, carry, s=s, step=step):
            at = pl.ds(pl.multiple_of(i * 16, 16), 16)
            total = send1[first, s, at].astype(F32)
            for k in range(3):
                total = total + recv1[k, s, at].astype(F32)
            if step:
                red[s, at] = total.astype(BF16)
            else:
                acc[at] = total
            return carry

        lax.fori_loop(0, 2 * quarter // 16, add, 0)
        if step:
            copy_two(step).start()
        if step == 1:
            first_part()
        if step == 3:
            second_part()

    for d in (1, 3, 2):
        w_swap(d).wait_recv()
        to_other((y + RING - d) % RING).start()
    dot_ref[...] = jnp.zeros_like(dot_ref)
    packed[...] = jnp.zeros_like(packed)

    def features(block):
        at = pl.ds(pl.multiple_of(block * (2 * shard), 128), 2 * shard)
        value = lax.dot_general(
            grad[...],
            w[pl.ds(pl.multiple_of(block * (2 * shard), 16), 2 * shard)],
            (((1,), (1,)), ((), ())),
            preferred_element_type=F32,
        )
        value = value * gain_ref[:, at]
        scaled[:, at] = value
        value = value * res[:, at].astype(F32)
        part = dot_ref[...]
        for k in range(2 * shard // 128):
            part = part + value[:, k * 128 : (k + 1) * 128]
        dot_ref[...] = part

    def from_other(yy):
        piece = w_rows(yy, zh, 1 - c)
        remote(piece, piece, wc_sem, (yy,), other).wait_recv()

    for e in (1, 3, 2):
        copy_two(e).wait_recv()

    def add_two(i, carry):
        at = pl.ds(pl.multiple_of(i * 16, 16), 16)
        total = acc[at]
        for k in range(3):
            total = total + recv2[k, at].astype(F32)
        acc[at] = total
        return carry

    lax.fori_loop(0, 2 * quarter // 16, add_two, 0)
    high, wide = 16 - rows, acc.shape[1] - BLOCK
    for k in range(DEPTH):
        at = k * rows
        packed[k, :rows] = acc[at : at + rows, :wide]
        packed[k, rows:, :BLOCK] = acc[at : at + high, wide:]
        packed[k, rows : 2 * rows - high, BLOCK : 2 * BLOCK] = acc[at + high : at + rows, wide:]
    for k in range(DEPTH):
        send3[k] = packed[k].astype(BF16)

    def copy_three(d):
        return remote(send3.at[(z + d) % DEPTH], recv3.at[d - 1], three_sem, (d - 1,), along_z(d))

    hear(2)
    distances = (8, 7, 9, 6, 10, 5, 11, 4, 12, 3, 13, 2, 14, 1, 15)
    for d in distances:
        copy_three(d).start()

    for d in (0, 1, 3, 2):
        yy = (y + RING - d) % RING
        from_other(yy)
        features(yy * 2 + zh)

    def from_other_far(yy):
        piece = w_rows(yy, lo, 1 - c)
        remote(piece, piece, wd_sem, (yy,), other).wait_recv()
        features(yy * 2 + lo)

    before = None
    for back in (0, 1, 3, 2):
        yy = (y + RING - back) % RING

        @pl.when(c == 0)
        def _(yy=yy):
            for d in (1, 3, 2):
                piece = w_piece(0, yy, (x + RING - d) % RING)
                remote(piece, piece, wx_sem, (d - 1, yy), along_x(d)).wait_recv()

        if back:

            @pl.when(c == 1)
            def _(yy=yy, back=back):
                piece = w_rows(yy, lo, 1)
                remote(piece, piece, wx_sem, (back - 1, 0), along_y(back)).wait_recv()

        to_other_far(yy).start()
        if before is not None:
            from_other_far(before)
        before = yy
    from_other_far(before)

    rinv = rinv_ref[:, :1]
    factor = jnp.sum(dot_ref[...], axis=1, keepdims=True) * (1.0 / width) * rinv * rinv
    dot_ref[...] = jnp.broadcast_to(factor, dot_ref.shape)

    def finish(i, carry):
        at = pl.ds(pl.multiple_of(i * 16, 16), 16)
        rinv, factor = rinv_ref[at], dot_ref[at]
        for k in range(width // BLOCK):
            lanes = slice(k * BLOCK, (k + 1) * BLOCK)
            out[at, lanes] = (
                (scaled[at, lanes] - res[at, lanes].astype(F32) * factor) * rinv
            ).astype(BF16)
        return carry

    lax.fori_loop(0, tokens // 16, finish, 0)

    place_of_rows = (lax.axis_index("node") * (RING * Z_LO) + lax.axis_index("group")) * rows
    lane = lax.broadcasted_iota(jnp.int32, (16, width), 1)
    row = lax.broadcasted_iota(jnp.int32, (16, width), 0)
    own_gain = jnp.sum(
        jnp.where(lane == row + place_of_rows, gain_ref[...], 0.0), axis=1, keepdims=True
    )
    scale = float(tokens * RING * RING * DEPTH * 2) ** (-0.5)

    for d in distances:
        copy_three(d).wait_recv()
    total = send3[z].astype(F32)
    for k in range(DEPTH - 1):
        total = total + recv3[k].astype(F32)
    packed[0] = total
    factor = (own_gain * scale)[:rows]
    wg_ref[:, :wide] = packed[0, :rows] * factor
    wg_ref[:high, wide:] = packed[0, rows:, :BLOCK] * factor[:high]
    wg_ref[high:, wide:] = packed[0, rows : 2 * rows - high, BLOCK : 2 * BLOCK] * factor[high:]

    swap_grad.wait_send()
    for b in range(8):
        swap_res(b).wait_send()
    @pl.when(sends_far)
    def _():
        for j in range(REACH):
            w_far(j).wait_send()

    for d in (1, 2, 3):
        w_near(d).wait_send()
        w_swap(d).wait_send()
        w_side(d).wait_send()
        copy_two(d).wait_send()
        for s in range(RING):
            copy_one(d, s).wait_send()

    @pl.when(c == 0)
    def _():
        for d in (1, 2, 3):
            for yy in range(RING):
                w_across(d, yy).wait_send()

    @pl.when(c == 1)
    def _():
        for d in (1, 2, 3):
            w_whole(d).wait_send()

    for yy in range(RING):
        to_other(yy).wait_send()
        to_other_far(yy).wait_send()
    for d in distances:
        copy_three(d).wait_send()


def on_device(residual, norm_gain_vector, key_projection_matrix, key_output_gradient):
    tokens, width = residual.shape
    features = key_output_gradient.shape[1]
    shard = key_projection_matrix.shape[0]
    quarter = shard // RING
    hbm = pl.BlockSpec(memory_space=pltpu.HBM)
    vmem = pl.BlockSpec(memory_space=pltpu.VMEM)
    return pl.pallas_call(
        kernel,
        out_shape=(
            pltpu.VMEM((tokens, width), BF16),
            pltpu.VMEM((shard // (RING * Z_LO), features), F32),
        ),
        in_specs=[hbm, hbm, hbm, vmem],
        out_specs=(vmem, vmem),
        scratch_shapes=[
            pltpu.VMEM((tokens, width), BF16),
            pltpu.VMEM((tokens, features), BF16),
            pltpu.VMEM((8, 2 * tokens, 384), BF16),
            pltpu.VMEM((2 * tokens, features), BF16),
            pltpu.VMEM((8, 384, 2 * tokens), BF16),
            pltpu.VMEM((RING, RING, 2 * quarter, features), BF16),
            pltpu.VMEM((3, RING, 2 * quarter, features), BF16),
            pltpu.VMEM((RING, 2 * quarter, features), BF16),
            pltpu.VMEM((3, 2 * quarter, features), BF16),
            pltpu.VMEM((2 * quarter, features), F32),
            pltpu.VMEM((DEPTH, 16, features - BLOCK), F32),
            pltpu.VMEM((DEPTH, 16, features - BLOCK), BF16),
            pltpu.VMEM((DEPTH - 1, 16, features - BLOCK), BF16),
            pltpu.VMEM((width, features), BF16),
            pltpu.VMEM((tokens, width), F32),
            pltpu.VMEM((tokens, 128), F32),
            pltpu.VMEM((tokens, 128), F32),
            pltpu.SemaphoreType.DMA((11,)),
            pltpu.SemaphoreType.DMA((2, 9)),
            pltpu.SemaphoreType.DMA((2, 3, RING)),
            pltpu.SemaphoreType.DMA((2, 3)),
            pltpu.SemaphoreType.DMA((2, DEPTH - 1)),
            pltpu.SemaphoreType.REGULAR((3,)),
            pltpu.SemaphoreType.DMA((2, REACH)),
            pltpu.SemaphoreType.DMA((2, 3)),
            pltpu.SemaphoreType.DMA((2, 3)),
            pltpu.SemaphoreType.DMA((2, 3)),
            pltpu.SemaphoreType.DMA((2, 3, RING)),
            pltpu.SemaphoreType.DMA((2, RING)),
            pltpu.SemaphoreType.DMA((2, RING)),
        ],
        compiler_params=pltpu.CompilerParams(
            collective_id=0, has_side_effects=True, vmem_limit_bytes=54 * 2**20
        ),
        name="key_backward",
    )(residual, key_output_gradient, key_projection_matrix, norm_gain_vector.reshape(1, width))


def solution(mesh):
    return jax.shard_map(
        on_device,
        mesh=mesh,
        in_specs=(P(("node", "group"), None), P(), P("node", None), P(("node", "group"), None)),
        out_specs=(P(("node", "group"), None), P(("node", "group"), None)),
        check_vma=False,
    )
```

```python
import jax
import jax.numpy as jnp
from jax import lax
from jax.experimental import pallas as pl
from jax.experimental.pallas import tpu as pltpu
from jax.sharding import PartitionSpec as P

MESH = pl.DeviceIdType.MESH
F32, BF16 = jnp.float32, jnp.bfloat16

RING = 4
DEPTH = 16
Z_LO = 8
BLOCK = 128
ORDER = (2, 1, 3, 0)
REACH = 4


def place():
    n, g = lax.axis_index("node"), lax.axis_index("group")
    return g // Z_LO, n // 4, (n // 2) % 2 * Z_LO + g % Z_LO, n % 2


def device(x, y, z, c):
    return (y * 4 + z // Z_LO * 2 + c, x * Z_LO + z % Z_LO)


def kernel(
    res_hbm,
    grad_hbm,
    w_hbm,
    gain_ref,
    out,
    wg_ref,
    res,
    grad,
    both_res,
    both_grad,
    turned,
    send1,
    recv1,
    red,
    recv2,
    acc,
    packed,
    send3,
    recv3,
    w,
    scaled,
    rinv_ref,
    dot_ref,
    local_sem,
    pair_sem,
    one_sem,
    two_sem,
    three_sem,
    chain_sem,
    wz_sem,
    wa_sem,
    ws_sem,
    wb_sem,
    wx_sem,
    wc_sem,
    wd_sem,
):
    x, y, z, c = place()
    zh = z // Z_LO
    tokens, width = res.shape
    shard = w_hbm.shape[0]
    quarter = shard // RING
    rows = quarter // Z_LO
    first, second = x + c * (y - x), y + c * (x - y)
    other = device(x, y, z, 1 - c)

    def along_first(d):
        return device((x + (1 - c) * d) % RING, (y + c * d) % RING, z, c)

    def along_second(d):
        return device((x + c * d) % RING, (y + (1 - c) * d) % RING, z, c)

    def along_x(d):
        return device((x + d) % RING, y, z, c)

    def along_y(d):
        return device(x, (y + d) % RING, z, c)

    def along_z(d):
        return device(x, y, (z + d) % DEPTH, c)

    def remote(src, dst, sems, index, target):
        return pltpu.make_async_remote_copy(
            src_ref=src,
            dst_ref=dst,
            send_sem=sems.at[(0, *index)],
            recv_sem=sems.at[(1, *index)],
            device_id=target,
            device_id_type=MESH,
        )

    barrier = pltpu.get_barrier_semaphore()
    partners = (
        [along_z(d) for d in (1, 15)]
        + [along_x(d) for d in (1, 2, 3)]
        + [along_y(d) for d in (1, 2, 3)]
        + [other]
    )
    for partner in partners:
        pl.semaphore_signal(barrier, inc=1, device_id=partner, device_id_type=MESH)

    def w_rows(yy, hi, core, count=shard, at=0):
        start = ((yy * 2 + hi) * 2 + core) * shard + at
        return w.at[pl.ds(pl.multiple_of(start, 16), count)]

    def columns(block, core):
        start = block * (2 * shard) + core * 256
        return res_hbm.at[:, pl.ds(pl.multiple_of(start, 128), 384)]

    mine = pl.ds(pl.multiple_of(c * tokens, 16), tokens)
    load_res = pltpu.make_async_copy(res_hbm, res, local_sem.at[0])
    load_grad = pltpu.make_async_copy(grad_hbm, grad, local_sem.at[1])
    load_w = pltpu.make_async_copy(w_hbm, w_rows(y, zh, c), local_sem.at[2])

    def load_pair(b):
        return pltpu.make_async_copy(columns(b, c), both_res.at[b, mine], local_sem.at[3 + b])

    load_res.start()
    load_grad.start()
    for b in range(8):
        load_pair(b).start()
    load_w.start()
    pl.semaphore_wait(barrier, len(partners))

    swap_grad = remote(both_grad.at[mine], both_grad.at[mine], pair_sem, (8,), other)

    def swap_res(b):
        return remote(columns(b, 1 - c), both_res.at[b, mine], pair_sem, (b,), other)

    for b in range(8):
        swap_res(b).start()

    half_shard = shard // 2
    parity = z % 2

    def w_out(start, count):
        return w_hbm.at[pl.ds(pl.multiple_of(start, 16), count)]

    def w_near(d):
        return remote(
            w_out(parity * half_shard, half_shard),
            w_rows(y, zh, c, half_shard, parity * half_shard),
            wa_sem,
            (d - 1,),
            along_y(d),
        )

    def w_swap(d):
        piece = w_rows((y + RING - d) % RING, zh, c, half_shard, parity * half_shard)
        return remote(piece, piece, ws_sem, (d - 1,), device(x, y, z + 1 - 2 * parity, c))

    for d in (2, 1, 3):
        w_near(d).start()

    def tell(k):
        for d in (1 << k, DEPTH - (1 << k)):
            pl.semaphore_signal(chain_sem.at[k], inc=1, device_id=along_z(d), device_id_type=MESH)

    def hear(k):
        pl.semaphore_wait(chain_sem.at[k], 2)

    tell(0)
    load_grad.wait()
    load_res.wait()
    hear(0)
    tell(1)

    def square(i, total):
        for k in range(4):
            v = res[:, pl.ds(pl.multiple_of(i * 512 + k * 128, 128), 128)].astype(F32)
            total = total + v * v
        return total

    squares = lax.fori_loop(0, width // 512, square, jnp.zeros((tokens, 128), F32))
    rinv = 1.0 / jnp.sqrt(jnp.sum(squares, axis=1, keepdims=True) / width + 1e-06)
    rinv_ref[...] = jnp.broadcast_to(rinv, (tokens, 128))
    both_grad[mine] = (grad[...].astype(F32) * rinv).astype(BF16)

    swap_grad.start()
    load_w.wait()

    def to_other(yy):
        return remote(w_rows(yy, zh, c), w_rows(yy, zh, c), wc_sem, (yy,), other)

    to_other(y).start()

    z_lo = z % Z_LO
    sends_far = (z_lo == 0) | (z_lo == Z_LO - 1)

    def w_far(j):
        target = (z + DEPTH + jnp.where(z_lo == 0, -1 - j, 1 + j)) % DEPTH
        return pltpu.make_async_remote_copy(
            src_ref=w_out(x * quarter, quarter),
            dst_ref=w_rows(y, zh, c, quarter, x * quarter),
            send_sem=wz_sem.at[0, j],
            recv_sem=wz_sem.at[1, 0],
            device_id=device(x, y, target, c),
            device_id_type=MESH,
        )

    hear(1)

    @pl.when(sends_far)
    def _():
        for j in range(REACH - 1, -1, -1):
            w_far(j).start()

    tell(2)

    def turn(b, carry):
        load_pair(b).wait()
        swap_res(b).wait_recv()
        turned[b] = both_res[b].T
        return carry

    lax.fori_loop(0, 8, turn, 0)
    swap_grad.wait_recv()

    halves = (pl.ds(0, quarter), pl.ds(quarter, quarter))
    up, down, opposite = (first + 1) % RING, (first + 3) % RING, (first + 2) % RING

    def hop(k, s):
        block, slot, half, target = (
            (opposite, 2, 0, 1),
            (opposite, 2, 1, 3),
            (up, 0, 1, 1),
            (down, 1, 0, 3),
            (up, 0, 0, 1),
            (down, 1, 1, 3),
        )[k]
        return remote(
            send1.at[block, s, halves[half]],
            recv1.at[slot, s, halves[half]],
            one_sem,
            (k, s),
            along_first(target),
        )

    def relay(s):
        hop(0, s).wait_recv()
        hop(1, s).wait_recv()

        def join(i, carry):
            low = pl.ds(pl.multiple_of(i * 16, 16), 16)
            high = pl.ds(pl.multiple_of(quarter + i * 16, 16), 16)
            send1[up, s, low] = (send1[up, s, low].astype(F32) + recv1[2, s, low].astype(F32)).astype(BF16)
            send1[down, s, high] = (
                send1[down, s, high].astype(F32) + recv1[2, s, high].astype(F32)
            ).astype(BF16)
            return carry

        lax.fori_loop(0, quarter // 16, join, 0)
        hop(4, s).start()
        hop(5, s).start()

    def partial_block(yy):
        def half(hi, carry):
            value = jnp.dot(
                turned[yy * 2 + hi, pl.ds(pl.multiple_of(c * 64, 64), shard)],
                both_grad[...],
                preferred_element_type=F32,
            ).astype(BF16)
            for q in range(RING):
                send1[
                    q + c * (yy - q), yy + c * (q - yy), pl.ds(pl.multiple_of(hi * quarter, 16), quarter)
                ] = value[q * quarter : (q + 1) * quarter]
            return carry

        lax.fori_loop(0, 2, half, 0)

    for step in ORDER:
        yy = (y + step) % RING
        partial_block(yy)

        @pl.when(c == 0)
        def _(yy=yy):
            for k in range(4):
                hop(k, yy).start()

        @pl.when(c == 1)
        def _(step=step):
            for other_step in ORDER:
                for k in {2: (0, 1), 1: (2,), 3: (3,), 0: ()}[step]:
                    hop(k, (x + other_step) % RING).start()

    for d in (1, 3, 2):
        w_near(d).wait_recv()
        w_swap(d).start()

    lo = 1 - zh

    def w_piece(core, yy, xx):
        return w_rows(yy, lo, core, quarter, xx * quarter)

    def w_side(d):
        return remote(w_piece(c, y, x), w_piece(c, y, x), wb_sem, (d - 1,), along_second(d))

    def copy_two(e):
        return remote(red.at[(second + e) % RING], recv2.at[e - 1], two_sem, (e - 1,), along_second(e))

    def w_across(d, yy):
        piece = w_piece(0, yy, x)
        return remote(piece, piece, wx_sem, (d - 1, yy), along_x(d))

    def w_whole(d):
        piece = w_rows(y, lo, 1)
        return remote(piece, piece, wx_sem, (d - 1, 0), along_y(d))

    def to_other_far(yy):
        return remote(w_rows(yy, lo, c), w_rows(yy, lo, c), wd_sem, (yy,), other)

    def first_part():
        w_far(0).wait_recv()
        for d in (2, 1, 3):
            w_side(d).start()

    def second_part():
        for d in (1, 2, 3):
            w_side(d).wait_recv()

        @pl.when(c == 0)
        def _():
            for back in (0, 1, 3, 2):
                for d in (2, 1, 3):
                    w_across(d, (y + RING - back) % RING).start()

        @pl.when(c == 1)
        def _():
            for d in (1, 3, 2):
                w_whole(d).start()

    relay((second + ORDER[0]) % RING)
    for place_in_order, step in enumerate(ORDER):
        s = (second + step) % RING
        if place_in_order < RING - 1:
            relay((second + ORDER[place_in_order + 1]) % RING)
        for k in range(2, 6):
            hop(k, s).wait_recv()

        def add(i, carry, s=s, step=step):
            at = pl.ds(pl.multiple_of(i * 16, 16), 16)
            total = send1[first, s, at].astype(F32)
            for k in range(2):
                total = total + recv1[k, s, at].astype(F32)
            if step:
                red[s, at] = total.astype(BF16)
            else:
                acc[at] = total
            return carry

        lax.fori_loop(0, 2 * quarter // 16, add, 0)
        if step:
            copy_two(step).start()
        if step == 1:
            first_part()
        if step == 3:
            second_part()

    for d in (1, 3, 2):
        w_swap(d).wait_recv()
        to_other((y + RING - d) % RING).start()
    dot_ref[...] = jnp.zeros_like(dot_ref)
    packed[...] = jnp.zeros_like(packed)

    def features(block):
        at = pl.ds(pl.multiple_of(block * (2 * shard), 128), 2 * shard)
        value = lax.dot_general(
            grad[...],
            w[pl.ds(pl.multiple_of(block * (2 * shard), 16), 2 * shard)],
            (((1,), (1,)), ((), ())),
            preferred_element_type=F32,
        )
        value = value * gain_ref[:, at]
        scaled[:, at] = value
        value = value * res[:, at].astype(F32)
        part = dot_ref[...]
        for k in range(2 * shard // 128):
            part = part + value[:, k * 128 : (k + 1) * 128]
        dot_ref[...] = part

    def from_other(yy):
        piece = w_rows(yy, zh, 1 - c)
        remote(piece, piece, wc_sem, (yy,), other).wait_recv()

    for e in (1, 3, 2):
        copy_two(e).wait_recv()

    def add_two(i, carry):
        at = pl.ds(pl.multiple_of(i * 16, 16), 16)
        total = acc[at]
        for k in range(3):
            total = total + recv2[k, at].astype(F32)
        acc[at] = total
        return carry

    lax.fori_loop(0, 2 * quarter // 16, add_two, 0)
    high, wide = 16 - rows, acc.shape[1] - BLOCK
    for k in range(DEPTH):
        at = k * rows
        packed[k, :rows] = acc[at : at + rows, :wide]
        packed[k, rows:, :BLOCK] = acc[at : at + high, wide:]
        packed[k, rows : 2 * rows - high, BLOCK : 2 * BLOCK] = acc[at + high : at + rows, wide:]
    for k in range(DEPTH):
        send3[k] = packed[k].astype(BF16)

    def copy_three(d):
        return remote(send3.at[(z + d) % DEPTH], recv3.at[d - 1], three_sem, (d - 1,), along_z(d))

    hear(2)
    distances = (8, 7, 9, 6, 10, 5, 11, 4, 12, 3, 13, 2, 14, 1, 15)
    for d in distances:
        copy_three(d).start()

    for d in (0, 1, 3, 2):
        yy = (y + RING - d) % RING
        from_other(yy)
        features(yy * 2 + zh)

    def from_other_far(yy):
        piece = w_rows(yy, lo, 1 - c)
        remote(piece, piece, wd_sem, (yy,), other).wait_recv()
        features(yy * 2 + lo)

    before = None
    for back in (0, 1, 3, 2):
        yy = (y + RING - back) % RING

        @pl.when(c == 0)
        def _(yy=yy):
            for d in (1, 3, 2):
                piece = w_piece(0, yy, (x + RING - d) % RING)
                remote(piece, piece, wx_sem, (d - 1, yy), along_x(d)).wait_recv()

        if back:

            @pl.when(c == 1)
            def _(yy=yy, back=back):
                piece = w_rows(yy, lo, 1)
                remote(piece, piece, wx_sem, (back - 1, 0), along_y(back)).wait_recv()

        to_other_far(yy).start()
        if before is not None:
            from_other_far(before)
        before = yy
    from_other_far(before)

    rinv = rinv_ref[:, :1]
    factor = jnp.sum(dot_ref[...], axis=1, keepdims=True) * (1.0 / width) * rinv * rinv
    dot_ref[...] = jnp.broadcast_to(factor, dot_ref.shape)

    def finish(i, carry):
        at = pl.ds(pl.multiple_of(i * 16, 16), 16)
        rinv, factor = rinv_ref[at], dot_ref[at]
        for k in range(width // BLOCK):
            lanes = slice(k * BLOCK, (k + 1) * BLOCK)
            out[at, lanes] = (
                (scaled[at, lanes] - res[at, lanes].astype(F32) * factor) * rinv
            ).astype(BF16)
        return carry

    lax.fori_loop(0, tokens // 16, finish, 0)

    place_of_rows = (lax.axis_index("node") * (RING * Z_LO) + lax.axis_index("group")) * rows
    lane = lax.broadcasted_iota(jnp.int32, (16, width), 1)
    row = lax.broadcasted_iota(jnp.int32, (16, width), 0)
    own_gain = jnp.sum(
        jnp.where(lane == row + place_of_rows, gain_ref[...], 0.0), axis=1, keepdims=True
    )
    scale = float(tokens * RING * RING * DEPTH * 2) ** (-0.5)

    for d in distances:
        copy_three(d).wait_recv()
    total = send3[z].astype(F32)
    for k in range(DEPTH - 1):
        total = total + recv3[k].astype(F32)
    packed[0] = total
    factor = (own_gain * scale)[:rows]
    wg_ref[:, :wide] = packed[0, :rows] * factor
    wg_ref[:high, wide:] = packed[0, rows:, :BLOCK] * factor[:high]
    wg_ref[high:, wide:] = packed[0, rows : 2 * rows - high, BLOCK : 2 * BLOCK] * factor[high:]

    swap_grad.wait_send()
    for b in range(8):
        swap_res(b).wait_send()
    @pl.when(sends_far)
    def _():
        for j in range(REACH):
            w_far(j).wait_send()

    for d in (1, 2, 3):
        w_near(d).wait_send()
        w_swap(d).wait_send()
        w_side(d).wait_send()
        copy_two(d).wait_send()
        for s in range(RING):
            hop(d - 1, s).wait_send()
            hop(d + 2, s).wait_send()

    @pl.when(c == 0)
    def _():
        for d in (1, 2, 3):
            for yy in range(RING):
                w_across(d, yy).wait_send()

    @pl.when(c == 1)
    def _():
        for d in (1, 2, 3):
            w_whole(d).wait_send()

    for yy in range(RING):
        to_other(yy).wait_send()
        to_other_far(yy).wait_send()
    for d in distances:
        copy_three(d).wait_send()


def on_device(residual, norm_gain_vector, key_projection_matrix, key_output_gradient):
    tokens, width = residual.shape
    features = key_output_gradient.shape[1]
    shard = key_projection_matrix.shape[0]
    quarter = shard // RING
    hbm = pl.BlockSpec(memory_space=pltpu.HBM)
    vmem = pl.BlockSpec(memory_space=pltpu.VMEM)
    return pl.pallas_call(
        kernel,
        out_shape=(
            pltpu.VMEM((tokens, width), BF16),
            pltpu.VMEM((shard // (RING * Z_LO), features), F32),
        ),
        in_specs=[hbm, hbm, hbm, vmem],
        out_specs=(vmem, vmem),
        scratch_shapes=[
            pltpu.VMEM((tokens, width), BF16),
            pltpu.VMEM((tokens, features), BF16),
            pltpu.VMEM((8, 2 * tokens, 384), BF16),
            pltpu.VMEM((2 * tokens, features), BF16),
            pltpu.VMEM((8, 384, 2 * tokens), BF16),
            pltpu.VMEM((RING, RING, 2 * quarter, features), BF16),
            pltpu.VMEM((3, RING, 2 * quarter, features), BF16),
            pltpu.VMEM((RING, 2 * quarter, features), BF16),
            pltpu.VMEM((3, 2 * quarter, features), BF16),
            pltpu.VMEM((2 * quarter, features), F32),
            pltpu.VMEM((DEPTH, 16, features - BLOCK), F32),
            pltpu.VMEM((DEPTH, 16, features - BLOCK), BF16),
            pltpu.VMEM((DEPTH - 1, 16, features - BLOCK), BF16),
            pltpu.VMEM((width, features), BF16),
            pltpu.VMEM((tokens, width), F32),
            pltpu.VMEM((tokens, 128), F32),
            pltpu.VMEM((tokens, 128), F32),
            pltpu.SemaphoreType.DMA((11,)),
            pltpu.SemaphoreType.DMA((2, 9)),
            pltpu.SemaphoreType.DMA((2, 6, RING)),
            pltpu.SemaphoreType.DMA((2, 3)),
            pltpu.SemaphoreType.DMA((2, DEPTH - 1)),
            pltpu.SemaphoreType.REGULAR((3,)),
            pltpu.SemaphoreType.DMA((2, REACH)),
            pltpu.SemaphoreType.DMA((2, 3)),
            pltpu.SemaphoreType.DMA((2, 3)),
            pltpu.SemaphoreType.DMA((2, 3)),
            pltpu.SemaphoreType.DMA((2, 3, RING)),
            pltpu.SemaphoreType.DMA((2, RING)),
            pltpu.SemaphoreType.DMA((2, RING)),
        ],
        compiler_params=pltpu.CompilerParams(
            collective_id=0, has_side_effects=True, vmem_limit_bytes=54 * 2**20
        ),
        name="key_backward",
    )(residual, key_output_gradient, key_projection_matrix, norm_gain_vector.reshape(1, width))


def solution(mesh):
    return jax.shard_map(
        on_device,
        mesh=mesh,
        in_specs=(P(("node", "group"), None), P(), P("node", None), P(("node", "group"), None)),
        out_specs=(P(("node", "group"), None), P(("node", "group"), None)),
        check_vma=False,
    )
```

```python
import jax
import jax.numpy as jnp
from jax import lax
from jax.experimental import pallas as pl
from jax.experimental.pallas import tpu as pltpu
from jax.sharding import PartitionSpec as P

MESH = pl.DeviceIdType.MESH
F32, BF16 = jnp.float32, jnp.bfloat16

RING = 4
DEPTH = 16
Z_LO = 8
BLOCK = 128
ORDER = (2, 1, 3, 0)
REACH = 4


def place():
    n, g = lax.axis_index("node"), lax.axis_index("group")
    return g // Z_LO, n // 4, (n // 2) % 2 * Z_LO + g % Z_LO, n % 2


def device(x, y, z, c):
    return (y * 4 + z // Z_LO * 2 + c, x * Z_LO + z % Z_LO)


def kernel(
    res_hbm,
    grad_hbm,
    w_hbm,
    gain_ref,
    out,
    wg_ref,
    res,
    grad,
    both_res,
    both_grad,
    turned,
    send1,
    recv1,
    red,
    recv2,
    acc,
    packed,
    send3,
    recv3,
    w,
    scaled,
    rinv_ref,
    dot_ref,
    local_sem,
    pair_sem,
    one_sem,
    two_sem,
    three_sem,
    chain_sem,
    wz_sem,
    wa_sem,
    ws_sem,
    wb_sem,
    wx_sem,
    wc_sem,
    wd_sem,
):
    x, y, z, c = place()
    zh = z // Z_LO
    tokens, width = res.shape
    shard = w_hbm.shape[0]
    quarter = shard // RING
    rows = quarter // Z_LO
    first, second = x + c * (y - x), y + c * (x - y)
    other = device(x, y, z, 1 - c)

    def along_first(d):
        return device((x + (1 - c) * d) % RING, (y + c * d) % RING, z, c)

    def along_second(d):
        return device((x + c * d) % RING, (y + (1 - c) * d) % RING, z, c)

    def along_x(d):
        return device((x + d) % RING, y, z, c)

    def along_y(d):
        return device(x, (y + d) % RING, z, c)

    def along_z(d):
        return device(x, y, (z + d) % DEPTH, c)

    def remote(src, dst, sems, index, target):
        return pltpu.make_async_remote_copy(
            src_ref=src,
            dst_ref=dst,
            send_sem=sems.at[(0, *index)],
            recv_sem=sems.at[(1, *index)],
            device_id=target,
            device_id_type=MESH,
        )

    barrier = pltpu.get_barrier_semaphore()
    partners = (
        [along_z(d) for d in (1, 15)]
        + [along_x(d) for d in (1, 2, 3)]
        + [along_y(d) for d in (1, 2, 3)]
        + [other]
    )
    def w_rows(yy, hi, core, count=shard, at=0):
        start = ((yy * 2 + hi) * 2 + core) * shard + at
        return w.at[pl.ds(pl.multiple_of(start, 16), count)]

    def columns(block, core):
        start = block * (2 * shard) + core * 256
        return res_hbm.at[:, pl.ds(pl.multiple_of(start, 128), 384)]

    mine = pl.ds(pl.multiple_of(c * tokens, 16), tokens)
    load_res = pltpu.make_async_copy(res_hbm, res, local_sem.at[0])
    load_grad = pltpu.make_async_copy(grad_hbm, grad, local_sem.at[1])
    load_w = pltpu.make_async_copy(w_hbm, w_rows(y, zh, c), local_sem.at[2])

    def load_pair(b):
        return pltpu.make_async_copy(columns(b, c), both_res.at[b, mine], local_sem.at[3 + b])

    load_grad.start()
    load_res.start()
    for partner in partners:
        pl.semaphore_signal(barrier, inc=1, device_id=partner, device_id_type=MESH)
    for b in range(8):
        load_pair(b).start()
    load_w.start()
    pl.semaphore_wait(barrier, len(partners))

    swap_grad = remote(both_grad.at[mine], both_grad.at[mine], pair_sem, (8,), other)

    def swap_res(b):
        return remote(columns(b, 1 - c), both_res.at[b, mine], pair_sem, (b,), other)

    for b in range(8):
        swap_res(b).start()

    half_shard = shard // 2
    parity = z % 2

    def w_out(start, count):
        return w_hbm.at[pl.ds(pl.multiple_of(start, 16), count)]

    def w_near(d):
        return remote(
            w_out(parity * half_shard, half_shard),
            w_rows(y, zh, c, half_shard, parity * half_shard),
            wa_sem,
            (d - 1,),
            along_y(d),
        )

    def w_swap(d):
        piece = w_rows((y + RING - d) % RING, zh, c, half_shard, parity * half_shard)
        return remote(piece, piece, ws_sem, (d - 1,), device(x, y, z + 1 - 2 * parity, c))

    for d in (2, 1, 3):
        w_near(d).start()

    def tell(k):
        for d in (1 << k, DEPTH - (1 << k)):
            pl.semaphore_signal(chain_sem.at[k], inc=1, device_id=along_z(d), device_id_type=MESH)

    def hear(k):
        pl.semaphore_wait(chain_sem.at[k], 2)

    tell(0)
    load_grad.wait()
    load_res.wait()
    hear(0)
    tell(1)

    def square(i, total):
        for k in range(4):
            v = res[:, pl.ds(pl.multiple_of(i * 512 + k * 128, 128), 128)].astype(F32)
            total = total + v * v
        return total

    squares = lax.fori_loop(0, width // 512, square, jnp.zeros((tokens, 128), F32))
    rinv = 1.0 / jnp.sqrt(jnp.sum(squares, axis=1, keepdims=True) / width + 1e-06)
    rinv_ref[...] = jnp.broadcast_to(rinv, (tokens, 128))
    both_grad[mine] = (grad[...].astype(F32) * rinv).astype(BF16)

    swap_grad.start()
    load_w.wait()

    def to_other(yy):
        return remote(w_rows(yy, zh, c), w_rows(yy, zh, c), wc_sem, (yy,), other)

    to_other(y).start()

    z_lo = z % Z_LO
    sends_far = (z_lo == 0) | (z_lo == Z_LO - 1)

    def w_far(j):
        target = (z + DEPTH + jnp.where(z_lo == 0, -1 - j, 1 + j)) % DEPTH
        return pltpu.make_async_remote_copy(
            src_ref=w_out(x * quarter, quarter),
            dst_ref=w_rows(y, zh, c, quarter, x * quarter),
            send_sem=wz_sem.at[0, j],
            recv_sem=wz_sem.at[1, 0],
            device_id=device(x, y, target, c),
            device_id_type=MESH,
        )

    def far_out():
        hear(1)

        @pl.when(sends_far)
        def _():
            for j in range(REACH - 1, -1, -1):
                w_far(j).start()

        tell(2)


    def turn(b, carry):
        load_pair(b).wait()
        swap_res(b).wait_recv()
        turned[b] = both_res[b].T
        return carry

    lax.fori_loop(0, 8, turn, 0)
    swap_grad.wait_recv()

    halves = (pl.ds(0, quarter), pl.ds(quarter, quarter))
    up, down, opposite = (first + 1) % RING, (first + 3) % RING, (first + 2) % RING

    def hop(k, s):
        block, slot, half, target = (
            (opposite, 2, 0, 1),
            (opposite, 2, 1, 3),
            (up, 0, 1, 1),
            (down, 1, 0, 3),
            (up, 0, 0, 1),
            (down, 1, 1, 3),
        )[k]
        return remote(
            send1.at[block, s, halves[half]],
            recv1.at[slot, s, halves[half]],
            one_sem,
            (k, s),
            along_first(target),
        )

    def relay(s):
        hop(0, s).wait_recv()
        hop(1, s).wait_recv()

        def join(i, carry):
            low = pl.ds(pl.multiple_of(i * 16, 16), 16)
            high = pl.ds(pl.multiple_of(quarter + i * 16, 16), 16)
            send1[up, s, low] = (send1[up, s, low].astype(F32) + recv1[2, s, low].astype(F32)).astype(BF16)
            send1[down, s, high] = (
                send1[down, s, high].astype(F32) + recv1[2, s, high].astype(F32)
            ).astype(BF16)
            return carry

        lax.fori_loop(0, quarter // 16, join, 0)
        hop(4, s).start()
        hop(5, s).start()

    def partial_block(yy):
        def half(hi, carry):
            value = jnp.dot(
                turned[yy * 2 + hi, pl.ds(pl.multiple_of(c * 64, 64), shard)],
                both_grad[...],
                preferred_element_type=F32,
            ).astype(BF16)
            for q in range(RING):
                send1[
                    q + c * (yy - q), yy + c * (q - yy), pl.ds(pl.multiple_of(hi * quarter, 16), quarter)
                ] = value[q * quarter : (q + 1) * quarter]
            return carry

        lax.fori_loop(0, 2, half, 0)

    for step in ORDER:
        yy = (y + step) % RING
        partial_block(yy)

        @pl.when(c == 0)
        def _(yy=yy):
            for k in range(4):
                hop(k, yy).start()

        @pl.when(c == 1)
        def _(step=step):
            for other_step in ORDER:
                for k in {2: (0, 1), 1: (2,), 3: (3,), 0: ()}[step]:
                    hop(k, (x + other_step) % RING).start()

        if step == 2:
            far_out()

    for d in (1, 3, 2):
        w_near(d).wait_recv()
        w_swap(d).start()

    lo = 1 - zh

    def w_piece(core, yy, xx):
        return w_rows(yy, lo, core, quarter, xx * quarter)

    def w_side(d):
        return remote(w_piece(c, y, x), w_piece(c, y, x), wb_sem, (d - 1,), along_second(d))

    def copy_two(e):
        return remote(red.at[(second + e) % RING], recv2.at[e - 1], two_sem, (e - 1,), along_second(e))

    def w_across(d, yy):
        piece = w_piece(0, yy, x)
        return remote(piece, piece, wx_sem, (d - 1, yy), along_x(d))

    def w_whole(d):
        piece = w_rows(y, lo, 1)
        return remote(piece, piece, wx_sem, (d - 1, 0), along_y(d))

    def to_other_far(yy):
        return remote(w_rows(yy, lo, c), w_rows(yy, lo, c), wd_sem, (yy,), other)

    def first_part():
        w_far(0).wait_recv()
        for d in (2, 1, 3):
            w_side(d).start()

    def second_part():
        for d in (1, 2, 3):
            w_side(d).wait_recv()

        @pl.when(c == 0)
        def _():
            for back in (0, 1, 3, 2):
                for d in (2, 1, 3):
                    w_across(d, (y + RING - back) % RING).start()

        @pl.when(c == 1)
        def _():
            for d in (1, 3, 2):
                w_whole(d).start()

    relay((second + ORDER[0]) % RING)
    for place_in_order, step in enumerate(ORDER):
        s = (second + step) % RING
        if place_in_order < RING - 1:
            relay((second + ORDER[place_in_order + 1]) % RING)
        for k in range(2, 6):
            hop(k, s).wait_recv()

        def add(i, carry, s=s, step=step):
            at = pl.ds(pl.multiple_of(i * 16, 16), 16)
            total = send1[first, s, at].astype(F32)
            for k in range(2):
                total = total + recv1[k, s, at].astype(F32)
            if step:
                red[s, at] = total.astype(BF16)
            else:
                acc[at] = total
            return carry

        lax.fori_loop(0, 2 * quarter // 16, add, 0)
        if step:
            copy_two(step).start()
        if step == 2:
            first_part()
        if step == 3:
            second_part()

    for d in (1, 3, 2):
        w_swap(d).wait_recv()
        to_other((y + RING - d) % RING).start()
    dot_ref[...] = jnp.zeros_like(dot_ref)
    packed[...] = jnp.zeros_like(packed)

    def features(block):
        at = pl.ds(pl.multiple_of(block * (2 * shard), 128), 2 * shard)
        value = lax.dot_general(
            grad[...],
            w[pl.ds(pl.multiple_of(block * (2 * shard), 16), 2 * shard)],
            (((1,), (1,)), ((), ())),
            preferred_element_type=F32,
        )
        value = value * gain_ref[:, at]
        scaled[:, at] = value
        value = value * res[:, at].astype(F32)
        part = dot_ref[...]
        for k in range(2 * shard // 128):
            part = part + value[:, k * 128 : (k + 1) * 128]
        dot_ref[...] = part

    def from_other(yy):
        piece = w_rows(yy, zh, 1 - c)
        remote(piece, piece, wc_sem, (yy,), other).wait_recv()

    for e in (1, 3, 2):
        copy_two(e).wait_recv()

    def add_two(i, carry):
        at = pl.ds(pl.multiple_of(i * 16, 16), 16)
        total = acc[at]
        for k in range(3):
            total = total + recv2[k, at].astype(F32)
        acc[at] = total
        return carry

    lax.fori_loop(0, 2 * quarter // 16, add_two, 0)
    high, wide = 16 - rows, acc.shape[1] - BLOCK
    for k in range(DEPTH):
        at = k * rows
        packed[k, :rows] = acc[at : at + rows, :wide]
        packed[k, rows:, :BLOCK] = acc[at : at + high, wide:]
        packed[k, rows : 2 * rows - high, BLOCK : 2 * BLOCK] = acc[at + high : at + rows, wide:]
    for k in range(DEPTH):
        send3[k] = packed[k].astype(BF16)

    def copy_three(d):
        return remote(send3.at[(z + d) % DEPTH], recv3.at[d - 1], three_sem, (d - 1,), along_z(d))

    hear(2)
    distances = (8, 7, 9, 6, 10, 5, 11, 4, 12, 3, 13, 2, 14, 1, 15)
    for d in distances:
        copy_three(d).start()

    for d in (0, 1, 3, 2):
        yy = (y + RING - d) % RING
        from_other(yy)
        features(yy * 2 + zh)

    def from_other_far(yy):
        piece = w_rows(yy, lo, 1 - c)
        remote(piece, piece, wd_sem, (yy,), other).wait_recv()
        features(yy * 2 + lo)

    before = None
    for back in (0, 1, 3, 2):
        yy = (y + RING - back) % RING

        @pl.when(c == 0)
        def _(yy=yy):
            for d in (1, 3, 2):
                piece = w_piece(0, yy, (x + RING - d) % RING)
                remote(piece, piece, wx_sem, (d - 1, yy), along_x(d)).wait_recv()

        if back:

            @pl.when(c == 1)
            def _(yy=yy, back=back):
                piece = w_rows(yy, lo, 1)
                remote(piece, piece, wx_sem, (back - 1, 0), along_y(back)).wait_recv()

        to_other_far(yy).start()
        if before is not None:
            from_other_far(before)
        before = yy
    from_other_far(before)

    rinv = rinv_ref[:, :1]
    factor = jnp.sum(dot_ref[...], axis=1, keepdims=True) * (1.0 / width) * rinv * rinv
    dot_ref[...] = jnp.broadcast_to(factor, dot_ref.shape)

    def finish(i, carry):
        at = pl.ds(pl.multiple_of(i * 16, 16), 16)
        rinv, factor = rinv_ref[at], dot_ref[at]
        for k in range(width // BLOCK):
            lanes = slice(k * BLOCK, (k + 1) * BLOCK)
            out[at, lanes] = (
                (scaled[at, lanes] - res[at, lanes].astype(F32) * factor) * rinv
            ).astype(BF16)
        return carry

    lax.fori_loop(0, tokens // 16, finish, 0)

    place_of_rows = (lax.axis_index("node") * (RING * Z_LO) + lax.axis_index("group")) * rows
    lane = lax.broadcasted_iota(jnp.int32, (16, width), 1)
    row = lax.broadcasted_iota(jnp.int32, (16, width), 0)
    own_gain = jnp.sum(
        jnp.where(lane == row + place_of_rows, gain_ref[...], 0.0), axis=1, keepdims=True
    )
    scale = float(tokens * RING * RING * DEPTH * 2) ** (-0.5)

    for d in distances:
        copy_three(d).wait_recv()
    total = send3[z].astype(F32)
    for k in range(DEPTH - 1):
        total = total + recv3[k].astype(F32)
    packed[0] = total
    factor = (own_gain * scale)[:rows]
    wg_ref[:, :wide] = packed[0, :rows] * factor
    wg_ref[:high, wide:] = packed[0, rows:, :BLOCK] * factor[:high]
    wg_ref[high:, wide:] = packed[0, rows : 2 * rows - high, BLOCK : 2 * BLOCK] * factor[high:]

    swap_grad.wait_send()
    for b in range(8):
        swap_res(b).wait_send()
    @pl.when(sends_far)
    def _():
        for j in range(REACH):
            w_far(j).wait_send()

    for d in (1, 2, 3):
        w_near(d).wait_send()
        w_swap(d).wait_send()
        w_side(d).wait_send()
        copy_two(d).wait_send()
        for s in range(RING):
            hop(d - 1, s).wait_send()
            hop(d + 2, s).wait_send()

    @pl.when(c == 0)
    def _():
        for d in (1, 2, 3):
            for yy in range(RING):
                w_across(d, yy).wait_send()

    @pl.when(c == 1)
    def _():
        for d in (1, 2, 3):
            w_whole(d).wait_send()

    for yy in range(RING):
        to_other(yy).wait_send()
        to_other_far(yy).wait_send()
    for d in distances:
        copy_three(d).wait_send()


def on_device(residual, norm_gain_vector, key_projection_matrix, key_output_gradient):
    tokens, width = residual.shape
    features = key_output_gradient.shape[1]
    shard = key_projection_matrix.shape[0]
    quarter = shard // RING
    hbm = pl.BlockSpec(memory_space=pltpu.HBM)
    vmem = pl.BlockSpec(memory_space=pltpu.VMEM)
    return pl.pallas_call(
        kernel,
        out_shape=(
            pltpu.VMEM((tokens, width), BF16),
            pltpu.VMEM((shard // (RING * Z_LO), features), F32),
        ),
        in_specs=[hbm, hbm, hbm, vmem],
        out_specs=(vmem, vmem),
        scratch_shapes=[
            pltpu.VMEM((tokens, width), BF16),
            pltpu.VMEM((tokens, features), BF16),
            pltpu.VMEM((8, 2 * tokens, 384), BF16),
            pltpu.VMEM((2 * tokens, features), BF16),
            pltpu.VMEM((8, 384, 2 * tokens), BF16),
            pltpu.VMEM((RING, RING, 2 * quarter, features), BF16),
            pltpu.VMEM((3, RING, 2 * quarter, features), BF16),
            pltpu.VMEM((RING, 2 * quarter, features), BF16),
            pltpu.VMEM((3, 2 * quarter, features), BF16),
            pltpu.VMEM((2 * quarter, features), F32),
            pltpu.VMEM((DEPTH, 16, features - BLOCK), F32),
            pltpu.VMEM((DEPTH, 16, features - BLOCK), BF16),
            pltpu.VMEM((DEPTH - 1, 16, features - BLOCK), BF16),
            pltpu.VMEM((width, features), BF16),
            pltpu.VMEM((tokens, width), F32),
            pltpu.VMEM((tokens, 128), F32),
            pltpu.VMEM((tokens, 128), F32),
            pltpu.SemaphoreType.DMA((11,)),
            pltpu.SemaphoreType.DMA((2, 9)),
            pltpu.SemaphoreType.DMA((2, 6, RING)),
            pltpu.SemaphoreType.DMA((2, 3)),
            pltpu.SemaphoreType.DMA((2, DEPTH - 1)),
            pltpu.SemaphoreType.REGULAR((3,)),
            pltpu.SemaphoreType.DMA((2, REACH)),
            pltpu.SemaphoreType.DMA((2, 3)),
            pltpu.SemaphoreType.DMA((2, 3)),
            pltpu.SemaphoreType.DMA((2, 3)),
            pltpu.SemaphoreType.DMA((2, 3, RING)),
            pltpu.SemaphoreType.DMA((2, RING)),
            pltpu.SemaphoreType.DMA((2, RING)),
        ],
        compiler_params=pltpu.CompilerParams(
            collective_id=0, has_side_effects=True, vmem_limit_bytes=54 * 2**20
        ),
        name="key_backward",
    )(residual, key_output_gradient, key_projection_matrix, norm_gain_vector.reshape(1, width))


def solution(mesh):
    return jax.shard_map(
        on_device,
        mesh=mesh,
        in_specs=(P(("node", "group"), None), P(), P("node", None), P(("node", "group"), None)),
        out_specs=(P(("node", "group"), None), P(("node", "group"), None)),
        check_vma=False,
    )
```

```python
import jax
import jax.numpy as jnp
from jax import lax
from jax.experimental import pallas as pl
from jax.experimental.pallas import tpu as pltpu
from jax.sharding import PartitionSpec as P

MESH = pl.DeviceIdType.MESH
F32, BF16 = jnp.float32, jnp.bfloat16

RING = 4
DEPTH = 16
Z_LO = 8
BLOCK = 128
ORDER = (2, 1, 3, 0)
REACH = 4


def place():
    n, g = lax.axis_index("node"), lax.axis_index("group")
    return g // Z_LO, n // 4, (n // 2) % 2 * Z_LO + g % Z_LO, n % 2


def device(x, y, z, c):
    return (y * 4 + z // Z_LO * 2 + c, x * Z_LO + z % Z_LO)


def kernel(
    res_hbm,
    grad_hbm,
    w_hbm,
    gain_ref,
    out,
    wg_ref,
    res,
    grad,
    both_res,
    both_grad,
    turned,
    send1,
    recv1,
    red,
    recv2,
    acc,
    packed,
    send3,
    recv3,
    w,
    scaled,
    rinv_ref,
    dot_ref,
    local_sem,
    pair_sem,
    one_sem,
    two_sem,
    three_sem,
    chain_sem,
    wz_sem,
    wa_sem,
    ws_sem,
    wb_sem,
    wx_sem,
    wc_sem,
    wd_sem,
):
    x, y, z, c = place()
    zh = z // Z_LO
    tokens, width = res.shape
    shard = w_hbm.shape[0]
    quarter = shard // RING
    rows = quarter // Z_LO
    first, second = x + c * (y - x), y + c * (x - y)
    other = device(x, y, z, 1 - c)

    def along_first(d):
        return device((x + (1 - c) * d) % RING, (y + c * d) % RING, z, c)

    def along_second(d):
        return device((x + c * d) % RING, (y + (1 - c) * d) % RING, z, c)

    def along_x(d):
        return device((x + d) % RING, y, z, c)

    def along_y(d):
        return device(x, (y + d) % RING, z, c)

    def along_z(d):
        return device(x, y, (z + d) % DEPTH, c)

    def remote(src, dst, sems, index, target):
        return pltpu.make_async_remote_copy(
            src_ref=src,
            dst_ref=dst,
            send_sem=sems.at[(0, *index)],
            recv_sem=sems.at[(1, *index)],
            device_id=target,
            device_id_type=MESH,
        )

    barrier = pltpu.get_barrier_semaphore()
    partners = (
        [along_z(d) for d in (1, 15)]
        + [along_x(d) for d in (1, 2, 3)]
        + [along_y(d) for d in (1, 2, 3)]
        + [other]
    )
    def w_rows(yy, hi, core, count=shard, at=0):
        start = ((yy * 2 + hi) * 2 + core) * shard + at
        return w.at[pl.ds(pl.multiple_of(start, 16), count)]

    def columns(block, core):
        start = block * (2 * shard) + core * 256
        return res_hbm.at[:, pl.ds(pl.multiple_of(start, 128), 384)]

    mine = pl.ds(pl.multiple_of(c * tokens, 16), tokens)
    load_res = pltpu.make_async_copy(res_hbm, res, local_sem.at[0])
    load_grad = pltpu.make_async_copy(grad_hbm, grad, local_sem.at[1])
    load_w = pltpu.make_async_copy(w_hbm, w_rows(y, zh, c), local_sem.at[2])

    def load_pair(b):
        return pltpu.make_async_copy(columns(b, c), both_res.at[b, mine], local_sem.at[3 + b])

    load_grad.start()
    load_res.start()
    for partner in partners:
        pl.semaphore_signal(barrier, inc=1, device_id=partner, device_id_type=MESH)
    for b in range(8):
        load_pair(b).start()
    load_w.start()
    pl.semaphore_wait(barrier, len(partners))

    swap_grad = remote(both_grad.at[mine], both_grad.at[mine], pair_sem, (8,), other)

    def swap_res(b):
        return remote(columns(b, 1 - c), both_res.at[b, mine], pair_sem, (b,), other)

    for b in range(8):
        swap_res(b).start()

    half_shard = shard // 2
    parity = z % 2

    def w_out(start, count):
        return w_hbm.at[pl.ds(pl.multiple_of(start, 16), count)]

    def w_near(d):
        return remote(
            w_out(parity * half_shard, half_shard),
            w_rows(y, zh, c, half_shard, parity * half_shard),
            wa_sem,
            (d - 1,),
            along_y(d),
        )

    def w_swap(d):
        piece = w_rows((y + RING - d) % RING, zh, c, half_shard, parity * half_shard)
        return remote(piece, piece, ws_sem, (d - 1,), device(x, y, z + 1 - 2 * parity, c))

    for d in (2, 1, 3):
        w_near(d).start()

    def tell(k):
        for d in (1 << k, DEPTH - (1 << k)):
            pl.semaphore_signal(chain_sem.at[k], inc=1, device_id=along_z(d), device_id_type=MESH)

    def hear(k):
        pl.semaphore_wait(chain_sem.at[k], 2)

    tell(0)
    load_grad.wait()
    load_res.wait()
    hear(0)
    tell(1)

    def square(i, total):
        for k in range(4):
            v = res[:, pl.ds(pl.multiple_of(i * 512 + k * 128, 128), 128)].astype(F32)
            total = total + v * v
        return total

    squares = lax.fori_loop(0, width // 512, square, jnp.zeros((tokens, 128), F32))
    rinv = 1.0 / jnp.sqrt(jnp.sum(squares, axis=1, keepdims=True) / width + 1e-06)
    rinv_ref[...] = jnp.broadcast_to(rinv, (tokens, 128))
    both_grad[mine] = (grad[...].astype(F32) * rinv).astype(BF16)

    swap_grad.start()
    load_w.wait()

    def to_other(yy):
        return remote(w_rows(yy, zh, c), w_rows(yy, zh, c), wc_sem, (yy,), other)

    to_other(y).start()

    z_lo = z % Z_LO
    sends_far = (z_lo == 0) | (z_lo == Z_LO - 1)

    def w_far(j):
        target = (z + DEPTH + jnp.where(z_lo == 0, -1 - j, 1 + j)) % DEPTH
        return pltpu.make_async_remote_copy(
            src_ref=w_out(x * quarter, quarter),
            dst_ref=w_rows(y, zh, c, quarter, x * quarter),
            send_sem=wz_sem.at[0, j],
            recv_sem=wz_sem.at[1, 0],
            device_id=device(x, y, target, c),
            device_id_type=MESH,
        )

    def far_out():
        hear(1)

        @pl.when(sends_far)
        def _():
            for j in range(REACH - 1, -1, -1):
                w_far(j).start()

        tell(2)


    def turn(b, carry):
        load_pair(b).wait()
        swap_res(b).wait_recv()
        turned[b] = both_res[b].T
        return carry

    lax.fori_loop(0, 8, turn, 0)
    swap_grad.wait_recv()

    halves = (pl.ds(0, quarter), pl.ds(quarter, quarter))
    up, down, opposite = (first + 1) % RING, (first + 3) % RING, (first + 2) % RING

    def hop(k, s):
        block, slot, half, target = (
            (opposite, 2, 0, 1),
            (opposite, 2, 1, 3),
            (up, 0, 1, 1),
            (down, 1, 0, 3),
            (up, 0, 0, 1),
            (down, 1, 1, 3),
        )[k]
        return remote(
            send1.at[block, s, halves[half]],
            recv1.at[slot, s, halves[half]],
            one_sem,
            (k, s),
            along_first(target),
        )

    def relay(s):
        hop(0, s).wait_recv()
        hop(1, s).wait_recv()

        def join(i, carry):
            low = pl.ds(pl.multiple_of(i * 16, 16), 16)
            high = pl.ds(pl.multiple_of(quarter + i * 16, 16), 16)
            send1[up, s, low] = (send1[up, s, low].astype(F32) + recv1[2, s, low].astype(F32)).astype(BF16)
            send1[down, s, high] = (
                send1[down, s, high].astype(F32) + recv1[2, s, high].astype(F32)
            ).astype(BF16)
            return carry

        lax.fori_loop(0, quarter // 16, join, 0)
        hop(4, s).start()
        hop(5, s).start()

    def partial_block(yy):
        def half(hi, carry):
            value = jnp.dot(
                turned[yy * 2 + hi, pl.ds(pl.multiple_of(c * 64, 64), shard)],
                both_grad[...],
                preferred_element_type=F32,
            ).astype(BF16)
            for q in range(RING):
                send1[
                    q + c * (yy - q), yy + c * (q - yy), pl.ds(pl.multiple_of(hi * quarter, 16), quarter)
                ] = value[q * quarter : (q + 1) * quarter]
            return carry

        lax.fori_loop(0, 2, half, 0)

    for step in ORDER:
        yy = (y + step) % RING
        partial_block(yy)

        @pl.when(c == 0)
        def _(yy=yy):
            for k in range(4):
                hop(k, yy).start()

        @pl.when(c == 1)
        def _(step=step):
            for other_step in ORDER:
                for k in {2: (0, 1), 1: (2,), 3: (3,), 0: ()}[step]:
                    hop(k, (x + other_step) % RING).start()

        if step == 2:
            far_out()


    lo = 1 - zh

    def w_piece(core, yy, xx):
        return w_rows(yy, lo, core, quarter, xx * quarter)

    def w_side(d):
        return remote(w_piece(c, y, x), w_piece(c, y, x), wb_sem, (d - 1,), along_second(d))

    def copy_two(e):
        return remote(red.at[(second + e) % RING], recv2.at[e - 1], two_sem, (e - 1,), along_second(e))

    def w_across(d, yy):
        piece = w_piece(0, yy, x)
        return remote(piece, piece, wx_sem, (d - 1, yy), along_x(d))

    def w_whole(d):
        piece = w_rows(y, lo, 1)
        return remote(piece, piece, wx_sem, (d - 1, 0), along_y(d))

    def to_other_far(yy):
        return remote(w_rows(yy, lo, c), w_rows(yy, lo, c), wd_sem, (yy,), other)

    def first_part():
        w_far(0).wait_recv()
        for d in (2, 1, 3):
            w_side(d).start()

    def second_part():
        for d in (1, 2, 3):
            w_side(d).wait_recv()

        @pl.when(c == 0)
        def _():
            for back in (0, 1, 3, 2):
                for d in (2, 1, 3):
                    w_across(d, (y + RING - back) % RING).start()

        @pl.when(c == 1)
        def _():
            for d in (1, 3, 2):
                w_whole(d).start()

    relay((second + ORDER[0]) % RING)
    for d in (1, 3, 2):
        w_near(d).wait_recv()
        w_swap(d).start()
    for place_in_order, step in enumerate(ORDER):
        s = (second + step) % RING
        if place_in_order < RING - 1:
            relay((second + ORDER[place_in_order + 1]) % RING)
        for k in range(2, 6):
            hop(k, s).wait_recv()

        def add(i, carry, s=s, step=step):
            at = pl.ds(pl.multiple_of(i * quarter, 16), quarter)
            total = send1[first, s, at].astype(F32)
            for k in range(2):
                total = total + recv1[k, s, at].astype(F32)
            if step:
                red[s, at] = total.astype(BF16)
            else:
                acc[at] = total
            return carry

        lax.fori_loop(0, 2, add, 0)
        if step:
            copy_two(step).start()
        if step == 2:
            first_part()
        if step == 3:
            second_part()

    for d in (1, 3, 2):
        w_swap(d).wait_recv()
        to_other((y + RING - d) % RING).start()
    dot_ref[...] = jnp.zeros_like(dot_ref)
    packed[...] = jnp.zeros_like(packed)

    def features(block):
        at = pl.ds(pl.multiple_of(block * (2 * shard), 128), 2 * shard)
        value = lax.dot_general(
            grad[...],
            w[pl.ds(pl.multiple_of(block * (2 * shard), 16), 2 * shard)],
            (((1,), (1,)), ((), ())),
            preferred_element_type=F32,
        )
        value = value * gain_ref[:, at]
        scaled[:, at] = value
        value = value * res[:, at].astype(F32)
        part = dot_ref[...]
        for k in range(2 * shard // 128):
            part = part + value[:, k * 128 : (k + 1) * 128]
        dot_ref[...] = part

    def from_other(yy):
        piece = w_rows(yy, zh, 1 - c)
        remote(piece, piece, wc_sem, (yy,), other).wait_recv()

    for e in (1, 3, 2):
        copy_two(e).wait_recv()

    def add_two(i, carry):
        at = pl.ds(pl.multiple_of(i * quarter, 16), quarter)
        total = acc[at]
        for k in range(3):
            total = total + recv2[k, at].astype(F32)
        acc[at] = total
        return carry

    lax.fori_loop(0, 2, add_two, 0)
    high, wide = 16 - rows, acc.shape[1] - BLOCK
    for k in range(DEPTH):
        at = k * rows
        packed[k, :rows] = acc[at : at + rows, :wide]
        packed[k, rows:, :BLOCK] = acc[at : at + high, wide:]
        packed[k, rows : 2 * rows - high, BLOCK : 2 * BLOCK] = acc[at + high : at + rows, wide:]
    for k in range(DEPTH):
        send3[k] = packed[k].astype(BF16)

    def copy_three(d):
        return remote(send3.at[(z + d) % DEPTH], recv3.at[d - 1], three_sem, (d - 1,), along_z(d))

    hear(2)
    distances = (8, 7, 9, 6, 10, 5, 11, 4, 12, 3, 13, 2, 14, 1, 15)
    for d in distances:
        copy_three(d).start()

    for d in (0, 1, 3, 2):
        yy = (y + RING - d) % RING
        from_other(yy)
        features(yy * 2 + zh)

    def from_other_far(yy):
        piece = w_rows(yy, lo, 1 - c)
        remote(piece, piece, wd_sem, (yy,), other).wait_recv()
        features(yy * 2 + lo)

    before = None
    for back in (0, 1, 3, 2):
        yy = (y + RING - back) % RING

        @pl.when(c == 0)
        def _(yy=yy):
            for d in (1, 3, 2):
                piece = w_piece(0, yy, (x + RING - d) % RING)
                remote(piece, piece, wx_sem, (d - 1, yy), along_x(d)).wait_recv()

        if back:

            @pl.when(c == 1)
            def _(yy=yy, back=back):
                piece = w_rows(yy, lo, 1)
                remote(piece, piece, wx_sem, (back - 1, 0), along_y(back)).wait_recv()

        to_other_far(yy).start()
        if before is not None:
            from_other_far(before)
        before = yy
    from_other_far(before)

    rinv = rinv_ref[:, :1]
    factor = jnp.sum(dot_ref[...], axis=1, keepdims=True) * (1.0 / width) * rinv * rinv
    dot_ref[...] = jnp.broadcast_to(factor, dot_ref.shape)

    def finish(i, carry):
        at = pl.ds(pl.multiple_of(i * 16, 16), 16)
        rinv, factor = rinv_ref[at], dot_ref[at]
        for k in range(width // BLOCK):
            lanes = slice(k * BLOCK, (k + 1) * BLOCK)
            out[at, lanes] = (
                (scaled[at, lanes] - res[at, lanes].astype(F32) * factor) * rinv
            ).astype(BF16)
        return carry

    lax.fori_loop(0, tokens // 16, finish, 0)

    place_of_rows = (lax.axis_index("node") * (RING * Z_LO) + lax.axis_index("group")) * rows
    lane = lax.broadcasted_iota(jnp.int32, (16, width), 1)
    row = lax.broadcasted_iota(jnp.int32, (16, width), 0)
    own_gain = jnp.sum(
        jnp.where(lane == row + place_of_rows, gain_ref[...], 0.0), axis=1, keepdims=True
    )
    scale = float(tokens * RING * RING * DEPTH * 2) ** (-0.5)

    for d in distances:
        copy_three(d).wait_recv()
    total = send3[z].astype(F32)
    for k in range(DEPTH - 1):
        total = total + recv3[k].astype(F32)
    packed[0] = total
    factor = (own_gain * scale)[:rows]
    wg_ref[:, :wide] = packed[0, :rows] * factor
    wg_ref[:high, wide:] = packed[0, rows:, :BLOCK] * factor[:high]
    wg_ref[high:, wide:] = packed[0, rows : 2 * rows - high, BLOCK : 2 * BLOCK] * factor[high:]

    swap_grad.wait_send()
    for b in range(8):
        swap_res(b).wait_send()
    @pl.when(sends_far)
    def _():
        for j in range(REACH):
            w_far(j).wait_send()

    for d in (1, 2, 3):
        w_near(d).wait_send()
        w_swap(d).wait_send()
        w_side(d).wait_send()
        copy_two(d).wait_send()
        for s in range(RING):
            hop(d - 1, s).wait_send()
            hop(d + 2, s).wait_send()

    @pl.when(c == 0)
    def _():
        for d in (1, 2, 3):
            for yy in range(RING):
                w_across(d, yy).wait_send()

    @pl.when(c == 1)
    def _():
        for d in (1, 2, 3):
            w_whole(d).wait_send()

    for yy in range(RING):
        to_other(yy).wait_send()
        to_other_far(yy).wait_send()
    for d in distances:
        copy_three(d).wait_send()


def on_device(residual, norm_gain_vector, key_projection_matrix, key_output_gradient):
    tokens, width = residual.shape
    features = key_output_gradient.shape[1]
    shard = key_projection_matrix.shape[0]
    quarter = shard // RING
    hbm = pl.BlockSpec(memory_space=pltpu.HBM)
    vmem = pl.BlockSpec(memory_space=pltpu.VMEM)
    return pl.pallas_call(
        kernel,
        out_shape=(
            pltpu.VMEM((tokens, width), BF16),
            pltpu.VMEM((shard // (RING * Z_LO), features), F32),
        ),
        in_specs=[hbm, hbm, hbm, vmem],
        out_specs=(vmem, vmem),
        scratch_shapes=[
            pltpu.VMEM((tokens, width), BF16),
            pltpu.VMEM((tokens, features), BF16),
            pltpu.VMEM((8, 2 * tokens, 384), BF16),
            pltpu.VMEM((2 * tokens, features), BF16),
            pltpu.VMEM((8, 384, 2 * tokens), BF16),
            pltpu.VMEM((RING, RING, 2 * quarter, features), BF16),
            pltpu.VMEM((3, RING, 2 * quarter, features), BF16),
            pltpu.VMEM((RING, 2 * quarter, features), BF16),
            pltpu.VMEM((3, 2 * quarter, features), BF16),
            pltpu.VMEM((2 * quarter, features), F32),
            pltpu.VMEM((DEPTH, 16, features - BLOCK), F32),
            pltpu.VMEM((DEPTH, 16, features - BLOCK), BF16),
            pltpu.VMEM((DEPTH - 1, 16, features - BLOCK), BF16),
            pltpu.VMEM((width, features), BF16),
            pltpu.VMEM((tokens, width), F32),
            pltpu.VMEM((tokens, 128), F32),
            pltpu.VMEM((tokens, 128), F32),
            pltpu.SemaphoreType.DMA((11,)),
            pltpu.SemaphoreType.DMA((2, 9)),
            pltpu.SemaphoreType.DMA((2, 6, RING)),
            pltpu.SemaphoreType.DMA((2, 3)),
            pltpu.SemaphoreType.DMA((2, DEPTH - 1)),
            pltpu.SemaphoreType.REGULAR((3,)),
            pltpu.SemaphoreType.DMA((2, REACH)),
            pltpu.SemaphoreType.DMA((2, 3)),
            pltpu.SemaphoreType.DMA((2, 3)),
            pltpu.SemaphoreType.DMA((2, 3)),
            pltpu.SemaphoreType.DMA((2, 3, RING)),
            pltpu.SemaphoreType.DMA((2, RING)),
            pltpu.SemaphoreType.DMA((2, RING)),
        ],
        compiler_params=pltpu.CompilerParams(
            collective_id=0, has_side_effects=True, vmem_limit_bytes=54 * 2**20
        ),
        name="key_backward",
    )(residual, key_output_gradient, key_projection_matrix, norm_gain_vector.reshape(1, width))


def solution(mesh):
    return jax.shard_map(
        on_device,
        mesh=mesh,
        in_specs=(P(("node", "group"), None), P(), P("node", None), P(("node", "group"), None)),
        out_specs=(P(("node", "group"), None), P(("node", "group"), None)),
        check_vma=False,
    )
```
